512 devices in a mesh: dom: 64 (over y_hi, x, z), dim: 8 (over y_lo, core).
Axes of the slice: x: 4, y: 8 (y_hi: 2, y_lo: 4; y = y_hi * 4 + y_lo), z: 8, core: 2. Of those that a mesh axis runs over, the one named last changes fastest.
Arguments:
- ent_re: float32 [200, 32768], P('dim', 'dom'), may hold values from -8 to 8
- ent_im: float32 [200, 32768], P('dim', 'dom'), may hold values from -8 to 8
- ent_acc: float32 [32768], P('dom'), may hold values from 0.001 to 0.1
- rel_re: float32 [200, 4096], P('dim'), may hold values from -2.5 to 2.5
- rel_im: float32 [200, 4096], P('dim'), may hold values from -2.5 to 2.5
- rel_acc: float32 [4096], replicated, may hold values from 0.001 to 0.1
- lhs_rows: int32 [128, 128], P('dom'), may hold values from 0 to 511
- rhs_rows: int32 [128, 128], P('dom'), may hold values from 0 to 511
- rel_ids: int32 [128, 128], P('dom'), may hold values from 0 to 4095
- neg_rows: int32 [128, 1000], P('dom'), may hold values from 0 to 511
- bucket_step: int32 [128], P('dom'), may hold values from 0 to 4
Outputs:
- new_ent_re: float32 [200, 32768], P('dim', 'dom')
- new_ent_im: float32 [200, 32768], P('dim', 'dom')
- new_ent_acc: float32 [32768], P('dom')
- new_rel_re: float32 [200, 4096], P('dim')
- new_rel_im: float32 [200, 4096], P('dim')
- new_rel_acc: float32 [4096], replicated
The draws below stay inside these ranges and needn't reach their ends.
Inputs may be any that keep to these rules, and one draw needn't show every extreme that they name: bucket_step equal to 4 marks an empty slot.
All inputs are finite; a program needn't handle non-finite values.
Results may differ from the reference program's by a relative error of at most 0.0003.
Values sent between devices are 32-bit elements; how exact they have to be, the bound alone decides.
No kernel may reach another device: no remote copies, remote signals or barrier semaphores. Data moves between devices by JAX's collectives and lax.ppermute only.
A program may use at most 64 MiB of HBM per device.

```python
import math
import jax
import jax.numpy as jnp
import numpy as np
from jax import lax

D = 400
HALF = 200
REL = 4096
NEG = 1000
CH = 128
ROWS = 512
GROUPS = 2
STEPS = 4
ENTS = 32768
SLOTS = 128


def entity_values(key):
    base = jnp.clip(jax.random.normal(key, (HALF, ENTS), jnp.float32), -4.0, 4.0)
    return base * 0.5


def draw_ent_re(key, part):
    key = jax.random.fold_in(key, 11)
    return entity_values(key)


def draw_ent_im(key, part):
    key = jax.random.fold_in(key, 23)
    return entity_values(key)


def place_ends(entries, key, smallest, high):
    place = [jax.random.randint(jax.random.fold_in(key, axis), (), 0, length) for axis, length in enumerate(entries.shape)]
    longest = entries.shape.index(max(entries.shape))
    beside = place[:longest] + [(place[longest] + 1) % entries.shape[longest]] + place[longest + 1:]
    return entries.at[tuple(place)].set(smallest).at[tuple(beside)].set(high)


def level_of(own_key, shape, pieces, low, largest):
    gain, own = 1.0, jax.random.fold_in(own_key, 6)
    for dim, shards_of in pieces:
        draws = jnp.exp(jax.random.uniform(jax.random.fold_in(own, dim), (shards_of,), jnp.float32, low / len(pieces), largest / len(pieces)))
        gain = gain * jnp.repeat(draws, shape[dim] // shards_of).reshape([-1 if axis == dim else 1 for axis in range(len(shape))])
    return gain


def cumulative_ranks(number_of, slope):
    weights = [(1 << 20) // math.isqrt(standing ** slope) + 1 for standing in range(1, number_of + 1)]
    deviation = 1 + sum(weights) // (1 << 30)
    return np.cumsum(np.array([max(1, weight // deviation) for weight in weights]))


def ranked(key, extent, number_of, skew):
    listing = cumulative_ranks(number_of, skew)
    ticket = jax.random.randint(jax.random.fold_in(key, 1), extent, 0, int(listing[number_of - 1]))
    rank = jnp.searchsorted(jnp.asarray(listing, jnp.int32), ticket, side="right")
    return jax.random.permutation(jax.random.fold_in(key, 2), number_of)[rank].astype(jnp.int32)


def bell_draw(own_key, shape, deviation, reach, pieces=(), held_as=jnp.bfloat16):
    values = jax.random.normal(own_key, shape, jnp.float32) * deviation
    if len(pieces) > 0:
        values = level_of(own_key, shape, pieces, -0.22, 0.18) * values
    return jnp.clip(values, min=-reach, max=reach).astype(held_as)


def setup_inputs(seed: int = 0) -> dict:
    key_list = jax.random.split(jax.random.key(seed), 12)
    ent_re = draw_ent_re(jax.random.fold_in(key_list[11], 71), 0)
    ent_im = draw_ent_im(jax.random.fold_in(key_list[11], 71), 0)
    ent_acc = jnp.clip(jnp.exp(math.log(0.1) - 4.6051702 * jax.random.uniform(key_list[2], (ENTS,), jnp.float32) ** level_of(key_list[2], (ENTS,), ((0, 64),), -0.2, 0.2)), 0.001, 0.1)
    rel_re = bell_draw(key_list[3], (HALF, REL), 0.42, 2.5, ((0, 8),), jnp.float32)
    rel_im = bell_draw(key_list[4], (HALF, REL), 0.42, 2.5, ((0, 8),), jnp.float32)
    rel_acc = jnp.clip(jnp.exp(jax.random.uniform(key_list[5], (REL,), jnp.float32, math.log(0.001), math.log(0.1))), 0.001, 0.1)
    lhs_rows = place_ends(jax.random.randint(key_list[6], (SLOTS, CH), 0, ROWS), jax.random.fold_in(key_list[6], 1), 0, ROWS - 1).astype(jnp.int32)
    rhs_rows = place_ends(jax.random.randint(key_list[7], (SLOTS, CH), 0, ROWS), jax.random.fold_in(key_list[7], 1), 0, ROWS - 1).astype(jnp.int32)
    rel_ids = place_ends(ranked(key_list[8], (SLOTS, CH), REL, 2), jax.random.fold_in(key_list[8], 3), 0, REL - 1).astype(jnp.int32)
    neg_rows = place_ends(jax.random.randint(key_list[9], (SLOTS, NEG), 0, ROWS), jax.random.fold_in(key_list[9], 1), 0, ROWS - 1).astype(jnp.int32)
    bucket_step = place_ends(ranked(key_list[10], (SLOTS,), STEPS + 1, 2), jax.random.fold_in(key_list[10], 3), 0, STEPS).astype(jnp.int32)
    return dict(ent_re=ent_re, ent_im=ent_im, ent_acc=ent_acc, rel_re=rel_re, rel_im=rel_im, rel_acc=rel_acc, lhs_rows=lhs_rows, rhs_rows=rhs_rows, rel_ids=rel_ids, neg_rows=neg_rows, bucket_step=bucket_step)


learn_rate = 0.1

def reference(ent_re, ent_im, ent_acc, rel_re, rel_im, rel_acc, lhs_rows, rhs_rows, rel_ids, neg_rows, bucket_step):
    ent_re = ent_re.T
    ent_im = ent_im.T
    rel_re = rel_re.T
    rel_im = rel_im.T
    parts = ENTS // ROWS
    holder = jnp.arange(SLOTS, dtype=jnp.int32) // GROUPS
    live = (bucket_step < STEPS).astype(jnp.float32)
    stepc = jnp.minimum(bucket_step, STEPS - 1).astype(jnp.int32)
    target = (holder - stepc) % parts
    lhs_glob = lhs_rows + (holder * ROWS)[:, None]
    rhs_glob = rhs_rows + (target * ROWS)[:, None]
    neg_glob = neg_rows + (target * ROWS)[:, None]
    h_re, h_im = (ent_re[lhs_glob], ent_im[lhs_glob])
    r_re, r_im = (rel_re[rel_ids], rel_im[rel_ids])
    t_re, t_im = (ent_re[rhs_glob], ent_im[rhs_glob])
    n_re, n_im = (ent_re[neg_glob], ent_im[neg_glob])
    q_re = h_re * r_re - h_im * r_im
    q_im = h_re * r_im + h_im * r_re
    hp = lax.Precision.HIGHEST
    pos = lax.optimization_barrier(jnp.sum(q_re * t_re + q_im * t_im, -1))
    neg = jnp.einsum('cek,cnk->cen', q_re, n_re, precision=hp) + jnp.einsum('cek,cnk->cen', q_im, n_im, precision=hp)
    top = jnp.maximum(lax.optimization_barrier(jnp.max(neg, -1)), pos)
    e_pos = jnp.exp(pos - top)
    e_neg = jnp.exp(neg - top[..., None])
    denom = e_pos + lax.optimization_barrier(jnp.sum(e_neg, -1))
    w_pos = (e_pos / denom - 1.0) * live[:, None]
    w_neg = e_neg / denom[..., None] * live[:, None, None]
    gq_re = w_pos[..., None] * t_re + jnp.einsum('cen,cnk->cek', w_neg, n_re, precision=hp)
    gq_im = w_pos[..., None] * t_im + jnp.einsum('cen,cnk->cek', w_neg, n_im, precision=hp)
    gt_re, gt_im = (w_pos[..., None] * q_re, w_pos[..., None] * q_im)
    gn_re = jnp.einsum('cen,cek->cnk', w_neg, q_re, precision=hp)
    gn_im = jnp.einsum('cen,cek->cnk', w_neg, q_im, precision=hp)
    gh_re = gq_re * r_re + gq_im * r_im
    gh_im = gq_im * r_re - gq_re * r_im
    gr_re = gq_re * h_re + gq_im * h_im
    gr_im = gq_im * h_re - gq_re * h_im

    def scatter(values_a, ids_a, values_b, ids_b, values_c, ids_c):
        half = values_a.shape[-1]
        total = jax.ops.segment_sum(values_a.reshape(-1, half), ids_a.reshape(-1), ENTS)
        total = total + jax.ops.segment_sum(values_b.reshape(-1, half), ids_b.reshape(-1), ENTS)
        return total + jax.ops.segment_sum(values_c.reshape(-1, half), ids_c.reshape(-1), ENTS)
    g_re = scatter(gh_re, lhs_glob, gt_re, rhs_glob, gn_re, neg_glob)
    g_im = scatter(gh_im, lhs_glob, gt_im, rhs_glob, gn_im, neg_glob)
    rg_re = jax.ops.segment_sum(gr_re.reshape(-1, HALF), rel_ids.reshape(-1), REL)
    rg_im = jax.ops.segment_sum(gr_im.reshape(-1, HALF), rel_ids.reshape(-1), REL)
    new_ent_acc = ent_acc + lax.optimization_barrier(jnp.sum(g_re * g_re + g_im * g_im, -1)) / D
    new_rel_acc = rel_acc + lax.optimization_barrier(jnp.sum(rg_re * rg_re + rg_im * rg_im, -1)) / D
    ent_scale = learn_rate / jnp.sqrt(new_ent_acc)[:, None]
    rel_scale = learn_rate / jnp.sqrt(new_rel_acc)[:, None]
    return ((ent_re - ent_scale * g_re).T, (ent_im - ent_scale * g_im).T, new_ent_acc, (rel_re - rel_scale * rg_re).T, (rel_im - rel_scale * rg_im).T, new_rel_acc)
```

```python
import jax
import jax.numpy as jnp
from jax import lax
from jax.experimental import pallas as pl
from jax.experimental.pallas import tpu as pltpu
from jax.sharding import Mesh, PartitionSpec as P

D = 400
STEPS = 4
LEARN_RATE = 0.1
W = 25
ROWS = 512
CH = 128
REL = 4096
DOM = ("yh", "x", "z")
DIM = ("yl", "core")
ZY = ("yh", "z")
F32 = jnp.float32
BF16 = jnp.bfloat16
I32 = jnp.int32
HIGHEST = lax.Precision.HIGHEST
VM = pl.BlockSpec(memory_space=pltpu.VMEM)
SM = pl.BlockSpec(memory_space=pltpu.SMEM)


def call(kernel, name, outs, specs):
    single = isinstance(outs, tuple)
    shapes = [jax.ShapeDtypeStruct(s, F32) for s in ([outs] if single else outs)]
    return pl.pallas_call(
        kernel,
        out_shape=shapes[0] if single else shapes,
        in_specs=specs,
        out_specs=VM if single else [VM] * len(shapes),
        compiler_params=pltpu.CompilerParams(vmem_limit_bytes=32 * 1024 * 1024),
        name=name,
    )


def iota(shape, axis):
    return lax.broadcasted_iota(I32, shape, axis)


def split3(x):
    hi = x.astype(BF16)
    rest = x - hi.astype(F32)
    mid = rest.astype(BF16)
    lo = (rest - mid.astype(F32)).astype(BF16)
    return jnp.concatenate([hi, mid, lo], 0)


def join3(y):
    r = y.shape[0] // 3
    return y[:r] + (y[r : 2 * r] + y[2 * r :])


def nn(a, b):
    return lax.dot_general(a, b, (((1,), (0,)), ((), ())), preferred_element_type=F32)


def nt(a, b):
    return lax.dot_general(a, b, (((1,), (1,)), ((), ())), preferred_element_type=F32)


def onehot_rows(ids, count):
    return jnp.where(iota((count, ids.shape[1]), 0) == ids, 1.0, 0.0).astype(BF16)


def pad32(x):
    return jnp.concatenate([x, jnp.zeros((32 - W, x.shape[1]), F32)], 0)


def pack(block):
    return jnp.concatenate([pad32(block[:W]), pad32(block[W:])], 0)


def edge_ids(ref):
    return jnp.concatenate([ref[0:1, :], ref[1:2, :]], 1)


def query_kernel(info, ent_re, ent_im, rel_re, rel_im, racc, lhs, rel_ids, neg, head_o, relc_o, q_o, m_o, piece_o, pacc_o):
    own = jnp.concatenate([pad32(ent_re[...]), pad32(ent_im[...])], 0)
    head = join3(nn(split3(own), onehot_rows(edge_ids(lhs), ROWS)))
    ids = edge_ids(rel_ids)
    step = 1024
    acc = jnp.zeros((192, 2 * CH), F32)
    for k in range(0, REL, step):
        part = jnp.concatenate([pad32(rel_re[:, k : k + step]), pad32(rel_im[:, k : k + step])], 0)
        acc = acc + nn(split3(part), onehot_rows(ids - k, step))
    relc = join3(acc)
    head_o[...] = head
    relc_o[...] = relc
    h_re, h_im = head[:32], head[32:]
    r_re, r_im = relc[:32], relc[32:]
    q_o[...] = jnp.concatenate([h_re * r_re - h_im * r_im, h_re * r_im + h_im * r_re], 0)
    ones = jnp.ones((16, neg.shape[1]), BF16)
    for c in range(2):
        m_o[8 * c : 8 * c + 8, :] = nt(ones, onehot_rows(neg[c : c + 1, :], ROWS))[:8]
    p = info[2]
    tile = p // 2
    odd = p - 2 * tile
    lane = pl.multiple_of(tile * 128, 128)
    t_re = pad32(rel_re[:, pl.ds(lane, 128)])
    t_im = pad32(rel_im[:, pl.ds(lane, 128)])
    first = iota((32, 128), 1) < 64
    even_piece = jnp.where(first, t_re, pltpu.roll(t_im, 64, 1))
    odd_piece = jnp.where(first, pltpu.roll(t_re, 64, 1), t_im)
    piece_o[...] = jnp.where(odd == 0, even_piece, odd_piece)
    a = jnp.broadcast_to(racc[pl.ds(tile, 1), :], (8, 128))
    pacc_o[...] = jnp.where(odd == 0, a, pltpu.roll(a, 64, 1))


def choose(step, blocks):
    b = blocks[STEPS - 1]
    for s in range(STEPS - 1):
        b = jnp.where(step == s, blocks[s], b)
    return b


def score_kernel(bucket, q_r, b0, b1, b2, b3, s_o):
    blocks = [pack(b[...]) for b in (b0, b1, b2, b3)]
    for c in range(2):
        s = lax.dot_general(
            q_r[:, c * CH : (c + 1) * CH], choose(bucket[c], blocks),
            (((0,), (0,)), ((), ())), precision=HIGHEST, preferred_element_type=F32)
        for yl in range(4):
            s_o[2 * yl + c] = s[32 * yl : 32 * yl + 32]


def weight_kernel(info, bucket, parts, m_r, rhs, w_o):
    s = parts[0]
    for i in range(1, 8):
        s = s + parts[i]
    core = info[0]
    m = jnp.where(core == 0, m_r[0:1, :], m_r[8:9, :])
    live = jnp.where(jnp.where(core == 0, bucket[0], bucket[1]) < STEPS, 1.0, 0.0)
    hit = iota(s.shape, 1) == rhs[...]
    pos = jnp.sum(jnp.where(hit, s, 0.0), 1, keepdims=True)
    masked = jnp.where(m > 0.0, s, -1e30)
    top = jnp.maximum(jnp.max(masked, 1, keepdims=True), pos)
    e_pos = jnp.exp(pos - top)
    e_neg = m * jnp.exp(masked - top)
    denom = e_pos + jnp.sum(e_neg, 1, keepdims=True)
    w_pos = (e_pos / denom - 1.0) * live
    w = e_neg * (live / denom) + jnp.where(hit, w_pos, 0.0)
    for i in range(4):
        w_o[i] = w


def grad_kernel(info, bucket, q_r, head_r, relc_r, w_mine, w_other, b0, b1, b2, b3, lhs, rel_ids, s0_o, s1_o, s23_o, gr_o):
    core = info[0]
    mine = w_mine[...].reshape(CH, ROWS)
    other = w_other[...].reshape(CH, ROWS)
    blocks = [pack(b[...]) for b in (b0, b1, b2, b3)]
    gq = []
    slots = [jnp.zeros((64, ROWS), F32) for _ in range(STEPS)]
    for c in range(2):
        w = jnp.where(core == c, mine, other)
        step = jnp.minimum(bucket[c], STEPS - 1)
        block = choose(step, blocks)
        gq.append(lax.dot_general(block, w, (((1,), (1,)), ((), ())), precision=HIGHEST, preferred_element_type=F32))
        g = lax.dot_general(q_r[:, c * CH : (c + 1) * CH], w, (((1,), (0,)), ((), ())), precision=HIGHEST, preferred_element_type=F32)
        for s in range(STEPS):
            slots[s] = slots[s] + jnp.where(step == s, g, 0.0)
    gq = jnp.concatenate(gq, 1)
    g_re, g_im = gq[:32], gq[32:]
    h_re, h_im = head_r[:32, :], head_r[32:, :]
    r_re, r_im = relc_r[:32, :], relc_r[32:, :]
    gh = jnp.concatenate([g_re * r_re + g_im * r_im, g_im * r_re - g_re * r_im], 0)
    slots[0] = slots[0] + join3(nt(split3(gh), onehot_rows(edge_ids(lhs), ROWS)))
    gr_re = (g_re * h_re + g_im * h_im)[:W]
    gr_im = (g_im * h_re - g_re * h_im)[:W]
    ids = edge_ids(rel_ids).astype(F32)
    for i in range(4):
        gr_o[i, 0:W, :] = gr_re
        gr_o[i, W : 2 * W, :] = gr_im
        gr_o[i, 2 * W : 2 * W + 1, :] = ids
    for ref, at, slot in ((s0_o, 0, 0), (s1_o, 0, 1), (s23_o, 0, 3), (s23_o, 2 * W, 2)):
        ref[at : at + W, :] = slots[slot][:W]
        ref[at + W : at + 2 * W, :] = slots[slot][32 : 32 + W]


def place_kernel(info, gr, out):
    x = info[1]
    vals = []
    cols = []
    for i in range(4):
        vals.append(split3(pack(gr[i, 0 : 2 * W, :])))
        ids = gr[i, 2 * W : 2 * W + 1, :].astype(I32)
        mine = jnp.bitwise_and(jnp.right_shift(ids, 9), 3) == x
        cols.append(jnp.where(mine, jnp.right_shift(ids, 11) * 512 + jnp.bitwise_and(ids, 511), -1))
    total = join3(nt(jnp.concatenate(vals, 1), onehot_rows(jnp.concatenate(cols, 1), 1024)))
    first = iota((32, 128), 1) < 64
    for t in range(8):
        t_re = total[:32, 128 * t : 128 * t + 128]
        t_im = total[32:, 128 * t : 128 * t + 128]
        out[2 * t] = jnp.where(first, t_re, pltpu.roll(t_im, 64, 1))[:W]
        out[2 * t + 1] = jnp.where(first, pltpu.roll(t_re, 64, 1), t_im)[:W]


def square_kernel(parts, s0, got1, got23, tot_o, ent_o, sq_o):
    tot = parts[0]
    for i in range(1, 16):
        tot = tot + parts[i]
    tot_o[...] = tot
    rs = jnp.broadcast_to(jnp.sum(tot * tot, 0, keepdims=True), (8, 128))
    rs = (rs + pltpu.roll(rs, 64, 1))[0:1]
    ent = s0[...] + (got1[...] + got23[2 * W : 4 * W, :])
    ent_o[...] = ent
    es = jnp.sum(ent * ent, 0, keepdims=True)
    for i in range(8):
        sq_o[i, :, 0:ROWS] = es
        sq_o[i, :, ROWS : ROWS + 128] = rs


def update_kernel(sq, tot, ent, ent_re, ent_im, eacc, piece, pacc, re_o, im_o, acc_o, rel_o):
    s = sq[0]
    for i in range(1, 8):
        s = s + sq[i]
    acc = eacc[...] + s[:, :ROWS] / D
    acc_o[...] = acc
    scale = LEARN_RATE / jnp.sqrt(acc)
    re_o[...] = ent_re[...] - scale * ent[0:W, :]
    im_o[...] = ent_im[...] - scale * ent[W : 2 * W, :]
    racc = pacc[0:1, :] + s[:, ROWS:] / D
    racc = jnp.where(iota((1, 128), 1) < 64, racc, jnp.broadcast_to(pltpu.roll(jnp.broadcast_to(racc, (8, 128)), 64, 1)[0:1], (1, 128)))
    rel = piece[0:W, :] - (LEARN_RATE / jnp.sqrt(racc)) * tot[...]
    for i in range(64):
        rel_o[i, 0:W, :] = rel
        rel_o[i, W : W + 1, :] = racc


def unpack_kernel(rel, re_o, im_o, acc_o):
    first = iota((32, 128), 1) < 64
    pad = jnp.zeros((32 - W - 1, 128), F32)
    for t in range(32):
        a = jnp.concatenate([rel[2 * t], pad], 0)
        b = jnp.concatenate([rel[2 * t + 1], pad], 0)
        re = jnp.where(first, a, pltpu.roll(b, 64, 1))
        im = jnp.where(first, pltpu.roll(a, 64, 1), b)
        re_o[:, 128 * t : 128 * t + 128] = re[:W]
        im_o[:, 128 * t : 128 * t + 128] = im[:W]
        acc_o[t : t + 1, :] = re[W : W + 1]


def shift(block, distance):
    return lax.ppermute(block, DOM, [(i, (i + distance) % 64) for i in range(64)])


def exchange(pieces, axes):
    return lax.all_to_all(pieces, axes, 0, 0)


def per_device(ent_re, ent_im, ent_acc, rel_re, rel_im, rel_acc, lhs_rows, rhs_rows, rel_ids, neg_rows, bucket_step):
    core = lax.axis_index("core")
    yl = lax.axis_index("yl")
    info = jnp.stack([core, lax.axis_index("x"), lax.axis_index(DOM)]).astype(I32)
    own = jnp.concatenate([ent_re, ent_im], 0)
    b1, b2, b3 = [shift(own, d) for d in (1, 2, 3)]
    neg = jnp.pad(neg_rows, ((0, 0), (0, 24)), constant_values=-1)
    rhs = lax.dynamic_slice(rhs_rows, (core, 32 * yl), (1, 32)).reshape(32, 1)
    head, relc, q, m, piece, pacc = call(
        query_kernel, "query",
        [(64, 256), (64, 256), (64, 256), (16, ROWS), (32, 128), (8, 128)], [SM] + [VM] * 8,
    )(info, ent_re, ent_im, rel_re, rel_im, rel_acc.reshape(32, 128), lhs_rows, rel_ids, neg)
    s = call(score_kernel, "score", (8, 32, ROWS), [SM] + [VM] * 5)(bucket_step, q, own, b1, b2, b3)
    s = exchange(s, DIM)
    w = call(weight_kernel, "weight", (4, 32, ROWS), [SM, SM] + [VM] * 3)(info, bucket_step, s, m, rhs)
    w_mine = exchange(w, "yl")
    w_other = lax.ppermute(w_mine, "core", [(0, 1), (1, 0)])
    s0, s1, s23, gr = call(
        grad_kernel, "grad",
        [(2 * W, ROWS), (2 * W, ROWS), (4 * W, ROWS), (4, 2 * W + 1, 256)], [SM, SM] + [VM] * 11,
    )(info, bucket_step, q, head, relc, w_mine, w_other, own, b1, b2, b3, lhs_rows, rel_ids)
    got23 = shift(s23, -2)
    gr = exchange(gr, "x")
    pieces = call(place_kernel, "place", (16, W, 128), [SM, VM])(info, gr)
    got1 = shift(s1 + got23[: 2 * W], -1)
    pieces = exchange(pieces, ZY)
    tot, ent, sq = call(
        square_kernel, "square", [(W, 128), (2 * W, ROWS), (8, 1, ROWS + 128)], [VM] * 4
    )(pieces, s0, got1, got23)
    sq = exchange(sq, DIM)
    new_re, new_im, new_acc, rel = call(
        update_kernel, "update", [(W, ROWS), (W, ROWS), (1, ROWS), (64, W + 1, 128)], [VM] * 8
    )(sq, tot, ent, ent_re, ent_im, ent_acc.reshape(1, ROWS), piece, pacc)
    rel = exchange(rel, DOM)
    new_rel_re, new_rel_im, new_rel_acc = call(
        unpack_kernel, "unpack", [(W, REL), (W, REL), (32, 128)], [VM]
    )(rel)
    return new_re, new_im, new_acc.reshape(ROWS), new_rel_re, new_rel_im, new_rel_acc.reshape(REL)


def solution(mesh):
    fine = Mesh(mesh.devices.reshape(2, 4, 8, 4, 2), DOM + DIM)
    return jax.shard_map(
        per_device,
        mesh=fine,
        in_specs=(
            P(DIM, DOM), P(DIM, DOM), P(DOM), P(DIM, None), P(DIM, None), P(),
            P(DOM, None), P(DOM, None), P(DOM, None), P(DOM, None), P(DOM),
        ),
        out_specs=(P(DIM, DOM), P(DIM, DOM), P(DOM), P(DIM, None), P(DIM, None), P()),
        check_vma=False,
    )
```

```python
import jax
import jax.numpy as jnp
from jax import lax
from jax.experimental import pallas as pl
from jax.experimental.pallas import tpu as pltpu
from jax.sharding import Mesh, PartitionSpec as P

D = 400
STEPS = 4
LEARN_RATE = 0.1
W = 25
ROWS = 512
CH = 128
REL = 4096
DOM = ("yh", "x", "z")
DIM = ("yl", "core")
SWAP = [(0, 1), (1, 0)]
F32 = jnp.float32
BF16 = jnp.bfloat16
I32 = jnp.int32
HIGHEST = lax.Precision.HIGHEST
VM = pl.BlockSpec(memory_space=pltpu.VMEM)
SM = pl.BlockSpec(memory_space=pltpu.SMEM)


def call(kernel, name, outs, specs):
    single = isinstance(outs, tuple)
    shapes = [jax.ShapeDtypeStruct(s, F32) for s in ([outs] if single else outs)]
    return pl.pallas_call(
        kernel,
        out_shape=shapes[0] if single else shapes,
        in_specs=specs,
        out_specs=VM if single else [VM] * len(shapes),
        compiler_params=pltpu.CompilerParams(vmem_limit_bytes=32 * 1024 * 1024),
        name=name,
    )


def iota(shape, axis):
    return lax.broadcasted_iota(I32, shape, axis)


def split3(x):
    hi = x.astype(BF16)
    rest = x - hi.astype(F32)
    mid = rest.astype(BF16)
    lo = (rest - mid.astype(F32)).astype(BF16)
    return jnp.concatenate([hi, mid, lo], 0)


def join3(y):
    r = y.shape[0] // 3
    return y[:r] + (y[r : 2 * r] + y[2 * r :])


def nn(a, b):
    return lax.dot_general(a, b, (((1,), (0,)), ((), ())), preferred_element_type=F32)


def nt(a, b):
    return lax.dot_general(a, b, (((1,), (1,)), ((), ())), preferred_element_type=F32)


def onehot_rows(ids, count):
    return jnp.where(iota((count, ids.shape[1]), 0) == ids, 1.0, 0.0).astype(BF16)


def pad32(x):
    return jnp.concatenate([x, jnp.zeros((32 - W, x.shape[1]), F32)], 0)


def pack(block):
    return jnp.concatenate([pad32(block[:W]), pad32(block[W:])], 0)


def edge_ids(ref):
    return jnp.concatenate([ref[0:1, :], ref[1:2, :]], 1)


def query_kernel(ent_re, ent_im, rel_re, rel_im, lhs, rel_ids, neg, head_o, relc_o, q_o, m_o):
    own = jnp.concatenate([pad32(ent_re[...]), pad32(ent_im[...])], 0)
    head = join3(nn(split3(own), onehot_rows(edge_ids(lhs), ROWS)))
    ids = edge_ids(rel_ids)
    step = 1024
    acc = jnp.zeros((192, 2 * CH), F32)
    for k in range(0, REL, step):
        part = jnp.concatenate([pad32(rel_re[:, k : k + step]), pad32(rel_im[:, k : k + step])], 0)
        acc = acc + nn(split3(part), onehot_rows(ids - k, step))
    relc = join3(acc)
    head_o[...] = head
    relc_o[...] = relc
    h_re, h_im = head[:32], head[32:]
    r_re, r_im = relc[:32], relc[32:]
    q_o[...] = jnp.concatenate([h_re * r_re - h_im * r_im, h_re * r_im + h_im * r_re], 0)
    ones = jnp.ones((16, neg.shape[1]), BF16)
    for c in range(2):
        m_o[8 * c : 8 * c + 8, :] = nt(ones, onehot_rows(neg[c : c + 1, :], ROWS))[:8]


def choose(step, blocks):
    b = blocks[STEPS - 1]
    for s in range(STEPS - 1):
        b = jnp.where(step == s, blocks[s], b)
    return b


def score_kernel(info, bucket, q_r, b0, b1, b2, b3, keep_o, send_o):
    core = info[0]
    blocks = [pack(b[...]) for b in (b0, b1, b2, b3)]
    q = [q_r[:, 0:CH], q_r[:, CH : 2 * CH]]
    for first, out in ((1, send_o), (0, keep_o)):
        c = core ^ first
        s = lax.dot_general(
            jnp.where(c == 0, q[0], q[1]), choose(bucket[c], blocks),
            (((0,), (0,)), ((), ())), precision=HIGHEST, preferred_element_type=F32)
        for yl in range(4):
            out[yl] = s[32 * yl : 32 * yl + 32]


def add_kernel(a, b, o):
    o[...] = a[...] + b[...]


def weight_kernel(info, bucket, parts, m_r, rhs, w_o):
    s = parts[0]
    for i in range(1, 4):
        s = s + parts[i]
    core = info[0]
    m = jnp.where(core == 0, m_r[0:1, :], m_r[8:9, :])
    live = jnp.where(jnp.where(core == 0, bucket[0], bucket[1]) < STEPS, 1.0, 0.0)
    hit = iota(s.shape, 1) == rhs[...]
    pos = jnp.sum(jnp.where(hit, s, 0.0), 1, keepdims=True)
    masked = jnp.where(m > 0.0, s, -1e30)
    top = jnp.maximum(jnp.max(masked, 1, keepdims=True), pos)
    e_pos = jnp.exp(pos - top)
    e_neg = m * jnp.exp(masked - top)
    denom = e_pos + jnp.sum(e_neg, 1, keepdims=True)
    w_pos = (e_pos / denom - 1.0) * live
    w = e_neg * (live / denom) + jnp.where(hit, w_pos, 0.0)
    for i in range(4):
        w_o[i] = w


def grad_kernel(info, bucket, q_r, head_r, relc_r, w_mine, w_other, b0, b1, b2, b3, lhs, rel_ids, s0_o, s1_o, s23_o, gr_o):
    core = info[0]
    mine = w_mine[...].reshape(CH, ROWS)
    other = w_other[...].reshape(CH, ROWS)
    blocks = [pack(b[...]) for b in (b0, b1, b2, b3)]
    gq = []
    slots = [jnp.zeros((64, ROWS), F32) for _ in range(STEPS)]
    for c in range(2):
        w = jnp.where(core == c, mine, other)
        step = jnp.minimum(bucket[c], STEPS - 1)
        block = choose(step, blocks)
        gq.append(lax.dot_general(block, w, (((1,), (1,)), ((), ())), precision=HIGHEST, preferred_element_type=F32))
        g = lax.dot_general(q_r[:, c * CH : (c + 1) * CH], w, (((1,), (0,)), ((), ())), precision=HIGHEST, preferred_element_type=F32)
        for s in range(STEPS):
            slots[s] = slots[s] + jnp.where(step == s, g, 0.0)
    gq = jnp.concatenate(gq, 1)
    g_re, g_im = gq[:32], gq[32:]
    h_re, h_im = head_r[:32, :], head_r[32:, :]
    r_re, r_im = relc_r[:32, :], relc_r[32:, :]
    gh = jnp.concatenate([g_re * r_re + g_im * r_im, g_im * r_re - g_re * r_im], 0)
    slots[0] = slots[0] + join3(nt(split3(gh), onehot_rows(edge_ids(lhs), ROWS)))
    gr_re = (g_re * h_re + g_im * h_im)[:W]
    gr_im = (g_im * h_re - g_re * h_im)[:W]
    ids = edge_ids(rel_ids).astype(F32)
    for i in range(4):
        gr_o[i, 0:W, :] = gr_re
        gr_o[i, W : 2 * W, :] = gr_im
        gr_o[i, 2 * W : 2 * W + 1, :] = ids
    for ref, at, slot in ((s0_o, 0, 0), (s1_o, 0, 1), (s23_o, 0, 3), (s23_o, 2 * W, 2)):
        ref[at : at + W, :] = slots[slot][:W]
        ref[at + W : at + 2 * W, :] = slots[slot][32 : 32 + W]


def place_kernel(info, gr, out):
    x = info[1]
    vals = []
    cols = []
    for i in range(4):
        vals.append(split3(pack(gr[i, 0 : 2 * W, :])))
        ids = gr[i, 2 * W : 2 * W + 1, :].astype(I32)
        cols.append(jnp.where(jnp.right_shift(ids, 10) == x, jnp.bitwise_and(ids, 1023), -1))
    total = join3(nt(jnp.concatenate(vals, 1), onehot_rows(jnp.concatenate(cols, 1), 1024)))
    for z in range(8):
        out[z, 0:W, :] = total[:W, 128 * z : 128 * z + 128]
        out[z, W : 2 * W, :] = total[32 : 32 + W, 128 * z : 128 * z + 128]


def fold_kernel(parts, out):
    tot = parts[0]
    for i in range(1, 8):
        tot = tot + parts[i]
    out[...] = tot


def both_kernel(a, b, out):
    tot = a[...] + b[...]
    for z in range(8):
        out[z] = tot


def copies_kernel(a, out):
    for x in range(4):
        for z in range(8):
            out[x, 2 * W * z : 2 * W * z + 2 * W, :] = a[z]


def square_kernel(rel, s0, got1, got23, ent_o, sq_o):
    ent = s0[...] + (got1[...] + got23[2 * W : 4 * W, :])
    ent_o[...] = ent
    es = jnp.sum(ent * ent, 0, keepdims=True)
    for i in range(8):
        sq_o[i, :, 0:ROWS] = es
    for t in range(32):
        tot = rel[t // 8, 2 * W * (t % 8) : 2 * W * (t % 8) + 2 * W, :]
        rs = jnp.sum(tot * tot, 0, keepdims=True)
        for i in range(8):
            sq_o[i, :, ROWS + 128 * t : ROWS + 128 * t + 128] = rs


def update_kernel(sq, rel, ent, ent_re, ent_im, eacc, rel_re, rel_im, racc, re_o, im_o, acc_o, rre_o, rim_o, racc_o):
    s = sq[0]
    for i in range(1, 8):
        s = s + sq[i]
    acc = eacc[...] + s[:, :ROWS] / D
    acc_o[...] = acc
    scale = LEARN_RATE / jnp.sqrt(acc)
    re_o[...] = ent_re[...] - scale * ent[0:W, :]
    im_o[...] = ent_im[...] - scale * ent[W : 2 * W, :]
    acc = racc[...] + s[:, ROWS:] / D
    racc_o[...] = acc
    scale = LEARN_RATE / jnp.sqrt(acc)
    for t in range(32):
        at = slice(128 * t, 128 * t + 128)
        tot = rel[t // 8, 2 * W * (t % 8) : 2 * W * (t % 8) + 2 * W, :]
        rre_o[:, at] = rel_re[:, at] - scale[:, at] * tot[:W]
        rim_o[:, at] = rel_im[:, at] - scale[:, at] * tot[W:]


def shift(block, distance):
    return lax.ppermute(block, DOM, [(i, (i + distance) % 64) for i in range(64)])


def exchange(pieces, axes):
    return lax.all_to_all(pieces, axes, 0, 0)


def per_device(ent_re, ent_im, ent_acc, rel_re, rel_im, rel_acc, lhs_rows, rhs_rows, rel_ids, neg_rows, bucket_step):
    core = lax.axis_index("core")
    yl = lax.axis_index("yl")
    info = jnp.stack([core, lax.axis_index("x")]).astype(I32)
    own = jnp.concatenate([ent_re, ent_im], 0)
    b1, b2, b3 = [shift(own, d) for d in (1, 2, 3)]
    neg = jnp.pad(neg_rows, ((0, 0), (0, 24)), constant_values=-1)
    rhs = lax.dynamic_slice(rhs_rows, (core, 32 * yl), (1, 32)).reshape(32, 1)
    head, relc, q, m = call(
        query_kernel, "query", [(64, 256), (64, 256), (64, 256), (16, ROWS)], [VM] * 7,
    )(ent_re, ent_im, rel_re, rel_im, lhs_rows, rel_ids, neg)
    quarter = (4, 32, ROWS)
    keep, send = call(score_kernel, "score", [quarter, quarter], [SM, SM] + [VM] * 5)(info, bucket_step, q, own, b1, b2, b3)
    s = call(add_kernel, "add", quarter, [VM] * 2)(keep, lax.ppermute(send, "core", SWAP))
    s = exchange(s, "yl")
    w = call(weight_kernel, "weight", quarter, [SM, SM] + [VM] * 3)(info, bucket_step, s, m, rhs)
    w_mine = exchange(w, "yl")
    w_other = lax.ppermute(w_mine, "core", SWAP)
    s0, s1, s23, gr = call(
        grad_kernel, "grad",
        [(2 * W, ROWS), (2 * W, ROWS), (4 * W, ROWS), (4, 2 * W + 1, 256)], [SM, SM] + [VM] * 11,
    )(info, bucket_step, q, head, relc, w_mine, w_other, own, b1, b2, b3, lhs_rows, rel_ids)
    got23 = shift(s23, -2)
    gr = exchange(gr, "x")
    pieces = call(place_kernel, "place", (8, 2 * W, 128), [SM, VM])(info, gr)
    got1 = shift(s1 + got23[: 2 * W], -1)
    pieces = exchange(pieces, "z")
    half = call(fold_kernel, "fold", (2 * W, 128), [VM])(pieces)
    rel = call(both_kernel, "both", (8, 2 * W, 128), [VM] * 2)(half, lax.ppermute(half, "yh", SWAP))
    rel = exchange(rel, "z")
    rel = exchange(call(copies_kernel, "copies", (4, 16 * W, 128), [VM])(rel), "x")
    ent, sq = call(square_kernel, "square", [(2 * W, ROWS), (8, 1, ROWS + REL)], [VM] * 4)(rel, s0, got1, got23)
    sq = exchange(sq, DIM)
    new_re, new_im, new_acc, new_rel_re, new_rel_im, new_rel_acc = call(
        update_kernel, "update", [(W, ROWS), (W, ROWS), (1, ROWS), (W, REL), (W, REL), (1, REL)], [VM] * 9
    )(sq, rel, ent, ent_re, ent_im, ent_acc.reshape(1, ROWS), rel_re, rel_im, rel_acc.reshape(1, REL))
    return new_re, new_im, new_acc.reshape(ROWS), new_rel_re, new_rel_im, new_rel_acc.reshape(REL)


def solution(mesh):
    fine = Mesh(mesh.devices.reshape(2, 4, 8, 4, 2), DOM + DIM)
    return jax.shard_map(
        per_device,
        mesh=fine,
        in_specs=(
            P(DIM, DOM), P(DIM, DOM), P(DOM), P(DIM, None), P(DIM, None), P(),
            P(DOM, None), P(DOM, None), P(DOM, None), P(DOM, None), P(DOM),
        ),
        out_specs=(P(DIM, DOM), P(DIM, DOM), P(DOM), P(DIM, None), P(DIM, None), P()),
        check_vma=False,
    )
```

```python
import jax
import jax.numpy as jnp
from jax import lax
from jax.experimental import pallas as pl
from jax.experimental.pallas import tpu as pltpu
from jax.sharding import Mesh, PartitionSpec as P

D = 400
STEPS = 4
LEARN_RATE = 0.1
W = 25
ROWS = 512
CH = 128
REL = 4096
DOM = ("yh", "x", "z")
DIM = ("yl", "core")
SWAP = [(0, 1), (1, 0)]
F32 = jnp.float32
BF16 = jnp.bfloat16
I32 = jnp.int32
HIGHEST = lax.Precision.HIGHEST
VM = pl.BlockSpec(memory_space=pltpu.VMEM)
SM = pl.BlockSpec(memory_space=pltpu.SMEM)


def call(kernel, name, outs, specs):
    single = isinstance(outs, tuple)
    shapes = [jax.ShapeDtypeStruct(s, F32) for s in ([outs] if single else outs)]
    return pl.pallas_call(
        kernel,
        out_shape=shapes[0] if single else shapes,
        in_specs=specs,
        out_specs=VM if single else [VM] * len(shapes),
        compiler_params=pltpu.CompilerParams(vmem_limit_bytes=32 * 1024 * 1024),
        name=name,
    )


def iota(shape, axis):
    return lax.broadcasted_iota(I32, shape, axis)


def split3(x):
    hi = x.astype(BF16)
    rest = x - hi.astype(F32)
    mid = rest.astype(BF16)
    lo = (rest - mid.astype(F32)).astype(BF16)
    return jnp.concatenate([hi, mid, lo], 0)


def join3(y):
    r = y.shape[0] // 3
    return y[:r] + (y[r : 2 * r] + y[2 * r :])


def nn(a, b):
    return lax.dot_general(a, b, (((1,), (0,)), ((), ())), preferred_element_type=F32)


def nt(a, b):
    return lax.dot_general(a, b, (((1,), (1,)), ((), ())), preferred_element_type=F32)


def onehot_rows(ids, count):
    return jnp.where(iota((count, ids.shape[1]), 0) == ids, 1.0, 0.0).astype(BF16)


def pad32(x):
    return jnp.concatenate([x, jnp.zeros((32 - W, x.shape[1]), F32)], 0)


def pack(block):
    return jnp.concatenate([pad32(block[:W]), pad32(block[W:])], 0)


def edge_ids(ref):
    return jnp.concatenate([ref[0:1, :], ref[1:2, :]], 1)


def query_kernel(info, ent_re, ent_im, rel_re, rel_im, lhs, rhs, rel_ids, neg, head_o, relc_o, q_o, m_o, hit_o):
    own = jnp.concatenate([pad32(ent_re[...]), pad32(ent_im[...])], 0)
    head = join3(nn(split3(own), onehot_rows(edge_ids(lhs), ROWS)))
    ids = edge_ids(rel_ids)
    step = 1024
    acc = jnp.zeros((192, 2 * CH), F32)
    for k in range(0, REL, step):
        part = jnp.concatenate([pad32(rel_re[:, k : k + step]), pad32(rel_im[:, k : k + step])], 0)
        acc = acc + nn(split3(part), onehot_rows(ids - k, step))
    relc = join3(acc)
    head_o[...] = head
    relc_o[...] = relc
    h_re, h_im = head[:32], head[32:]
    r_re, r_im = relc[:32], relc[32:]
    q_o[...] = jnp.concatenate([h_re * r_re - h_im * r_im, h_re * r_im + h_im * r_re], 0)
    first = info[0] == 0
    ones = jnp.ones((16, neg.shape[1]), BF16)
    m_o[...] = nt(ones, onehot_rows(jnp.where(first, neg[0:1, :], neg[1:2, :]), ROWS))[:8]
    ids = jnp.where(first, rhs[0:1, :], rhs[1:2, :])
    hit_o[...] = jnp.transpose(jnp.where(iota((ROWS, CH), 0) == ids, 1.0, 0.0))


def choose(step, blocks):
    b = blocks[STEPS - 1]
    for s in range(STEPS - 1):
        b = jnp.where(step == s, blocks[s], b)
    return b


def score_kernel(info, bucket, q_r, b0, b1, b2, b3, keep_o, send_o):
    core = info[0]
    blocks = [pack(b[...]) for b in (b0, b1, b2, b3)]
    q = [q_r[:, 0:CH], q_r[:, CH : 2 * CH]]
    for first, out in ((1, send_o), (0, keep_o)):
        c = core ^ first
        s = lax.dot_general(
            jnp.where(c == 0, q[0], q[1]), choose(bucket[c], blocks),
            (((0,), (0,)), ((), ())), precision=HIGHEST, preferred_element_type=F32)
        for yl in range(4):
            out[yl] = s[32 * yl : 32 * yl + 32]


def add_kernel(a, b, o):
    o[...] = a[...] + b[...]


def weight_kernel(info, bucket, parts, m_r, hit_r, w_o):
    s = parts[0]
    for i in range(1, 4):
        s = s + parts[i]
    m = m_r[0:1, :]
    live = jnp.where(jnp.where(info[0] == 0, bucket[0], bucket[1]) < STEPS, 1.0, 0.0)
    hit = hit_r[pl.ds(pl.multiple_of(info[2] * 32, 32), 32), :] > 0.5
    pos = jnp.sum(jnp.where(hit, s, 0.0), 1, keepdims=True)
    masked = jnp.where(m > 0.0, s, -1e30)
    top = jnp.maximum(jnp.max(masked, 1, keepdims=True), pos)
    e_pos = jnp.exp(pos - top)
    e_neg = m * jnp.exp(masked - top)
    denom = e_pos + jnp.sum(e_neg, 1, keepdims=True)
    w_pos = (e_pos / denom - 1.0) * live
    w = e_neg * (live / denom) + jnp.where(hit, w_pos, 0.0)
    for i in range(4):
        w_o[i] = w


def grad_kernel(info, bucket, q_r, head_r, relc_r, w_mine, w_other, b0, b1, b2, b3, lhs, rel_ids, s0_o, s1_o, s2_o, s3_o, gr_o):
    core = info[0]
    mine = w_mine[...].reshape(CH, ROWS)
    other = w_other[...].reshape(CH, ROWS)
    blocks = [pack(b[...]) for b in (b0, b1, b2, b3)]
    gq = []
    slots = [jnp.zeros((64, ROWS), F32) for _ in range(STEPS)]
    for c in range(2):
        w = jnp.where(core == c, mine, other)
        step = jnp.minimum(bucket[c], STEPS - 1)
        block = choose(step, blocks)
        gq.append(lax.dot_general(block, w, (((1,), (1,)), ((), ())), precision=HIGHEST, preferred_element_type=F32))
        g = lax.dot_general(q_r[:, c * CH : (c + 1) * CH], w, (((1,), (0,)), ((), ())), precision=HIGHEST, preferred_element_type=F32)
        for s in range(STEPS):
            slots[s] = slots[s] + jnp.where(step == s, g, 0.0)
    gq = jnp.concatenate(gq, 1)
    g_re, g_im = gq[:32], gq[32:]
    h_re, h_im = head_r[:32, :], head_r[32:, :]
    r_re, r_im = relc_r[:32, :], relc_r[32:, :]
    gh = jnp.concatenate([g_re * r_re + g_im * r_im, g_im * r_re - g_re * r_im], 0)
    slots[0] = slots[0] + join3(nt(split3(gh), onehot_rows(edge_ids(lhs), ROWS)))
    gr_re = (g_re * h_re + g_im * h_im)[:W]
    gr_im = (g_im * h_re - g_re * h_im)[:W]
    ids = edge_ids(rel_ids).astype(F32)
    for i in range(4):
        gr_o[i, 0:W, :] = gr_re
        gr_o[i, W : 2 * W, :] = gr_im
        gr_o[i, 2 * W : 2 * W + 1, :] = ids
    for ref, slot in zip((s0_o, s1_o, s2_o, s3_o), slots):
        ref[0:W, :] = slot[:W]
        ref[W : 2 * W, :] = slot[32 : 32 + W]


def place_kernel(info, gr, out):
    x = info[1]
    vals = []
    cols = []
    for i in range(4):
        vals.append(split3(pack(gr[i, 0 : 2 * W, :])))
        ids = gr[i, 2 * W : 2 * W + 1, :].astype(I32)
        cols.append(jnp.where(jnp.right_shift(ids, 10) == x, jnp.bitwise_and(ids, 1023), -1))
    total = join3(nt(jnp.concatenate(vals, 1), onehot_rows(jnp.concatenate(cols, 1), 1024)))
    for z in range(8):
        out[z, 0:W, :] = total[:W, 128 * z : 128 * z + 128]
        out[z, W : 2 * W, :] = total[32 : 32 + W, 128 * z : 128 * z + 128]


def fold_kernel(parts, out):
    tot = parts[0]
    for i in range(1, 8):
        tot = tot + parts[i]
    out[...] = tot


def both_kernel(a, b, out):
    tot = a[...] + b[...]
    for i in range(32):
        out[i] = tot


def square_kernel(rel, s0, got1, got2, got3, ent_o, sq_o):
    ent = s0[...] + (got1[...] + (got2[...] + got3[...]))
    ent_o[...] = ent
    es = jnp.sum(ent * ent, 0, keepdims=True)
    for i in range(8):
        sq_o[i, :, 0:ROWS] = es
    for t in range(32):
        tot = rel[t]
        rs = jnp.sum(tot * tot, 0, keepdims=True)
        for i in range(8):
            sq_o[i, :, ROWS + 128 * t : ROWS + 128 * t + 128] = rs


def update_kernel(sq, rel, ent, ent_re, ent_im, eacc, rel_re, rel_im, racc, re_o, im_o, acc_o, rre_o, rim_o, racc_o):
    s = sq[0]
    for i in range(1, 8):
        s = s + sq[i]
    acc = eacc[...] + s[:, :ROWS] / D
    acc_o[...] = acc
    scale = LEARN_RATE / jnp.sqrt(acc)
    re_o[...] = ent_re[...] - scale * ent[0:W, :]
    im_o[...] = ent_im[...] - scale * ent[W : 2 * W, :]
    acc = racc[...] + s[:, ROWS:] / D
    racc_o[...] = acc
    scale = LEARN_RATE / jnp.sqrt(acc)
    for t in range(32):
        at = slice(128 * t, 128 * t + 128)
        tot = rel[t]
        rre_o[:, at] = rel_re[:, at] - scale[:, at] * tot[:W]
        rim_o[:, at] = rel_im[:, at] - scale[:, at] * tot[W:]


def shift(block, distance):
    return lax.ppermute(block, DOM, [(i, (i + distance) % 64) for i in range(64)])


def exchange(pieces, axes):
    return lax.all_to_all(pieces, axes, 0, 0)


def per_device(ent_re, ent_im, ent_acc, rel_re, rel_im, rel_acc, lhs_rows, rhs_rows, rel_ids, neg_rows, bucket_step):
    info = jnp.stack([lax.axis_index("core"), lax.axis_index("x"), lax.axis_index("yl")]).astype(I32)
    own = jnp.concatenate([ent_re, ent_im], 0)
    b1, b2, b3 = [shift(own, d) for d in (1, 2, 3)]
    neg = jnp.pad(neg_rows, ((0, 0), (0, 24)), constant_values=-1)
    head, relc, q, m, hit = call(
        query_kernel, "query", [(64, 256), (64, 256), (64, 256), (8, ROWS), (CH, ROWS)], [SM] + [VM] * 8,
    )(info, ent_re, ent_im, rel_re, rel_im, lhs_rows, rhs_rows, rel_ids, neg)
    quarter = (4, 32, ROWS)
    block = (2 * W, ROWS)
    keep, send = call(score_kernel, "score", [quarter, quarter], [SM, SM] + [VM] * 5)(info, bucket_step, q, own, b1, b2, b3)
    s = call(add_kernel, "add", quarter, [VM] * 2)(keep, lax.ppermute(send, "core", SWAP))
    s = exchange(s, "yl")
    w = call(weight_kernel, "weight", quarter, [SM, SM] + [VM] * 3)(info, bucket_step, s, m, hit)
    w_mine = exchange(w, "yl")
    w_other = lax.ppermute(w_mine, "core", SWAP)
    s0, s1, s2, s3, gr = call(
        grad_kernel, "grad", [block, block, block, block, (4, 2 * W + 1, 256)], [SM, SM] + [VM] * 11,
    )(info, bucket_step, q, head, relc, w_mine, w_other, own, b1, b2, b3, lhs_rows, rel_ids)
    got = [shift(s1, -1), shift(s2, -2), shift(s3, -3)]
    gr = exchange(gr, "x")
    pieces = call(place_kernel, "place", (8, 2 * W, 128), [SM, VM])(info, gr)
    half = call(fold_kernel, "fold", (2 * W, 128), [VM])(exchange(pieces, "z"))
    twin, got = lax.optimization_barrier((lax.ppermute(half, "yh", SWAP), got))
    rel = call(both_kernel, "both", (32, 2 * W, 128), [VM] * 2)(half, twin)
    rel = exchange(rel, ("x", "z"))
    ent, sq = call(square_kernel, "square", [block, (8, 1, ROWS + REL)], [VM] * 5)(rel, s0, *got)
    sq = exchange(sq, DIM)
    new_re, new_im, new_acc, new_rel_re, new_rel_im, new_rel_acc = call(
        update_kernel, "update", [(W, ROWS), (W, ROWS), (1, ROWS), (W, REL), (W, REL), (1, REL)], [VM] * 9
    )(sq, rel, ent, ent_re, ent_im, ent_acc.reshape(1, ROWS), rel_re, rel_im, rel_acc.reshape(1, REL))
    return new_re, new_im, new_acc.reshape(ROWS), new_rel_re, new_rel_im, new_rel_acc.reshape(REL)


def solution(mesh):
    fine = Mesh(mesh.devices.reshape(2, 4, 8, 4, 2), DOM + DIM)
    return jax.shard_map(
        per_device,
        mesh=fine,
        in_specs=(
            P(DIM, DOM), P(DIM, DOM), P(DOM), P(DIM, None), P(DIM, None), P(),
            P(DOM, None), P(DOM, None), P(DOM, None), P(DOM, None), P(DOM),
        ),
        out_specs=(P(DIM, DOM), P(DIM, DOM), P(DOM), P(DIM, None), P(DIM, None), P()),
        check_vma=False,
    )
```

```python
import jax
import jax.numpy as jnp
from jax import lax
from jax.experimental import pallas as pl
from jax.experimental.pallas import tpu as pltpu
from jax.sharding import Mesh, PartitionSpec as P

D = 400
STEPS = 4
LEARN_RATE = 0.1
W = 25
ROWS = 512
CH = 128
REL = 4096
DOM = ("yh", "x", "z")
DIM = ("yl", "core")
SWAP = [(0, 1), (1, 0)]
F32 = jnp.float32
BF16 = jnp.bfloat16
I32 = jnp.int32
HIGHEST = lax.Precision.HIGHEST
VM = pl.BlockSpec(memory_space=pltpu.VMEM)
SM = pl.BlockSpec(memory_space=pltpu.SMEM)


def call(kernel, name, outs, specs):
    single = isinstance(outs, tuple)
    shapes = [jax.ShapeDtypeStruct(s, F32) for s in ([outs] if single else outs)]
    return pl.pallas_call(
        kernel,
        out_shape=shapes[0] if single else shapes,
        in_specs=specs,
        out_specs=VM if single else [VM] * len(shapes),
        compiler_params=pltpu.CompilerParams(vmem_limit_bytes=32 * 1024 * 1024),
        name=name,
    )


def iota(shape, axis):
    return lax.broadcasted_iota(I32, shape, axis)


def split3(x):
    hi = x.astype(BF16)
    rest = x - hi.astype(F32)
    mid = rest.astype(BF16)
    lo = (rest - mid.astype(F32)).astype(BF16)
    return jnp.concatenate([hi, mid, lo], 0)


def join3(y):
    r = y.shape[0] // 3
    return y[:r] + (y[r : 2 * r] + y[2 * r :])


def nn(a, b):
    return lax.dot_general(a, b, (((1,), (0,)), ((), ())), preferred_element_type=F32)


def nt(a, b):
    return lax.dot_general(a, b, (((1,), (1,)), ((), ())), preferred_element_type=F32)


def onehot_rows(ids, count):
    return jnp.where(iota((count, ids.shape[1]), 0) == ids, 1.0, 0.0).astype(BF16)


def pad32(x):
    return jnp.concatenate([x, jnp.zeros((32 - W, x.shape[1]), F32)], 0)


def pack(block):
    return jnp.concatenate([pad32(block[:W]), pad32(block[W:])], 0)


def edge_ids(ref):
    return jnp.concatenate([ref[0:1, :], ref[1:2, :]], 1)


def query_kernel(info, ent_re, ent_im, rel_re, rel_im, lhs, rhs, rel_ids, neg, head_o, relc_o, q_o, m_o, hit_o):
    own = jnp.concatenate([pad32(ent_re[...]), pad32(ent_im[...])], 0)
    head = join3(nn(split3(own), onehot_rows(edge_ids(lhs), ROWS)))
    ids = edge_ids(rel_ids)
    step = 1024
    acc = jnp.zeros((192, 2 * CH), F32)
    for k in range(0, REL, step):
        part = jnp.concatenate([pad32(rel_re[:, k : k + step]), pad32(rel_im[:, k : k + step])], 0)
        acc = acc + nn(split3(part), onehot_rows(ids - k, step))
    relc = join3(acc)
    head_o[...] = head
    relc_o[...] = relc
    h_re, h_im = head[:32], head[32:]
    r_re, r_im = relc[:32], relc[32:]
    q_o[...] = jnp.concatenate([h_re * r_re - h_im * r_im, h_re * r_im + h_im * r_re], 0)
    first = info[0] == 0
    ones = jnp.ones((16, neg.shape[1]), BF16)
    m_o[...] = nt(ones, onehot_rows(jnp.where(first, neg[0:1, :], neg[1:2, :]), ROWS))[:8]
    ids = jnp.where(first, rhs[0:1, :], rhs[1:2, :])
    hit_o[...] = jnp.transpose(jnp.where(iota((ROWS, CH), 0) == ids, 1.0, 0.0))


def choose(step, blocks):
    b = blocks[STEPS - 1]
    for s in range(STEPS - 1):
        b = jnp.where(step == s, blocks[s], b)
    return b


def score_kernel(info, bucket, q_r, b0, b1, b2, b3, keep_o, send_o):
    core = info[0]
    blocks = [pack(b[...]) for b in (b0, b1, b2, b3)]
    q = [q_r[:, 0:CH], q_r[:, CH : 2 * CH]]
    for first, out in ((1, send_o), (0, keep_o)):
        c = core ^ first
        s = lax.dot_general(
            jnp.where(c == 0, q[0], q[1]), choose(bucket[c], blocks),
            (((0,), (0,)), ((), ())), precision=HIGHEST, preferred_element_type=F32)
        for yl in range(4):
            out[yl] = s[32 * yl : 32 * yl + 32]


def add_kernel(a, b, o):
    o[...] = a[...] + b[...]


def weight_kernel(info, bucket, parts, m_r, hit_r, w_o):
    s = parts[0]
    for i in range(1, 4):
        s = s + parts[i]
    m = m_r[0:1, :]
    live = jnp.where(jnp.where(info[0] == 0, bucket[0], bucket[1]) < STEPS, 1.0, 0.0)
    hit = hit_r[pl.ds(pl.multiple_of(info[2] * 32, 32), 32), :] > 0.5
    pos = jnp.sum(jnp.where(hit, s, 0.0), 1, keepdims=True)
    masked = jnp.where(m > 0.0, s, -1e30)
    top = jnp.maximum(jnp.max(masked, 1, keepdims=True), pos)
    e_pos = jnp.exp(pos - top)
    e_neg = m * jnp.exp(masked - top)
    denom = e_pos + jnp.sum(e_neg, 1, keepdims=True)
    w_pos = (e_pos / denom - 1.0) * live
    w = e_neg * (live / denom) + jnp.where(hit, w_pos, 0.0)
    for i in range(4):
        w_o[i] = w


def grad_kernel(info, bucket, q_r, head_r, relc_r, w_mine, w_other, b0, b1, b2, b3, lhs, rel_ids, s0_o, s1_o, s2_o, s3_o, gr_o):
    core = info[0]
    mine = w_mine[...].reshape(CH, ROWS)
    other = w_other[...].reshape(CH, ROWS)
    blocks = [pack(b[...]) for b in (b0, b1, b2, b3)]
    gq = []
    slots = [jnp.zeros((64, ROWS), F32) for _ in range(STEPS)]
    for c in range(2):
        w = jnp.where(core == c, mine, other)
        step = jnp.minimum(bucket[c], STEPS - 1)
        block = choose(step, blocks)
        gq.append(lax.dot_general(block, w, (((1,), (1,)), ((), ())), precision=HIGHEST, preferred_element_type=F32))
        g = lax.dot_general(q_r[:, c * CH : (c + 1) * CH], w, (((1,), (0,)), ((), ())), precision=HIGHEST, preferred_element_type=F32)
        for s in range(STEPS):
            slots[s] = slots[s] + jnp.where(step == s, g, 0.0)
    gq = jnp.concatenate(gq, 1)
    g_re, g_im = gq[:32], gq[32:]
    h_re, h_im = head_r[:32, :], head_r[32:, :]
    r_re, r_im = relc_r[:32, :], relc_r[32:, :]
    gh = jnp.concatenate([g_re * r_re + g_im * r_im, g_im * r_re - g_re * r_im], 0)
    slots[0] = slots[0] + join3(nt(split3(gh), onehot_rows(edge_ids(lhs), ROWS)))
    gr_re = (g_re * h_re + g_im * h_im)[:W]
    gr_im = (g_im * h_re - g_re * h_im)[:W]
    ids = edge_ids(rel_ids).astype(F32)
    for i in range(4):
        gr_o[i, 0:W, :] = gr_re
        gr_o[i, W : 2 * W, :] = gr_im
        gr_o[i, 2 * W : 2 * W + 1, :] = ids
    for ref, slot in zip((s0_o, s1_o, s2_o, s3_o), slots):
        ref[0:W, :] = slot[:W]
        ref[W : 2 * W, :] = slot[32 : 32 + W]


def place_kernel(info, gr, out):
    x = info[1]
    vals = []
    cols = []
    for i in range(4):
        vals.append(split3(pack(gr[i, 0 : 2 * W, :])))
        ids = gr[i, 2 * W : 2 * W + 1, :].astype(I32)
        cols.append(jnp.where(jnp.right_shift(ids, 10) == x, jnp.bitwise_and(ids, 1023), -1))
    total = join3(nt(jnp.concatenate(vals, 1), onehot_rows(jnp.concatenate(cols, 1), 1024)))
    for z in range(8):
        out[z, 0:W, :] = total[:W, 128 * z : 128 * z + 128]
        out[z, W : 2 * W, :] = total[32 : 32 + W, 128 * z : 128 * z + 128]


def fold_kernel(parts, out):
    tot = parts[0]
    for i in range(1, 8):
        tot = tot + parts[i]
    out[...] = tot


def both_kernel(a, b, s0, got1, got2, got3, out, ent_o, sq_o):
    tot = a[...] + b[...]
    for i in range(32):
        out[i] = tot
    ent = s0[...] + (got1[...] + (got2[...] + got3[...]))
    ent_o[...] = ent
    es = jnp.sum(ent * ent, 0, keepdims=True)
    rs = jnp.sum(tot * tot, 0, keepdims=True)
    for i in range(8):
        sq_o[i, :, 0:ROWS] = es
        sq_o[i, :, ROWS : ROWS + 128] = rs


def entity_kernel(info, sq, ent, ent_re, ent_im, eacc, racc, re_o, im_o, acc_o, racc_o):
    s = sq[0]
    for i in range(1, 8):
        s = s + sq[i]
    acc = racc[pl.ds(info[1] * 8 + info[3], 1), :] + s[:, ROWS:] / D
    for i in range(32):
        racc_o[i] = acc
    acc = eacc[...] + s[:, :ROWS] / D
    acc_o[...] = acc
    scale = LEARN_RATE / jnp.sqrt(acc)
    re_o[...] = ent_re[...] - scale * ent[0:W, :]
    im_o[...] = ent_im[...] - scale * ent[W : 2 * W, :]


def relation_kernel(rel, racc, rel_re, rel_im, re_o, im_o, acc_o):
    for t in range(32):
        at = slice(128 * t, 128 * t + 128)
        acc = racc[t]
        acc_o[t : t + 1, :] = acc
        scale = LEARN_RATE / jnp.sqrt(acc)
        tot = rel[t]
        re_o[:, at] = rel_re[:, at] - scale * tot[:W]
        im_o[:, at] = rel_im[:, at] - scale * tot[W:]


def shift(block, distance):
    return lax.ppermute(block, DOM, [(i, (i + distance) % 64) for i in range(64)])


def exchange(pieces, axes):
    return lax.all_to_all(pieces, axes, 0, 0)


def per_device(ent_re, ent_im, ent_acc, rel_re, rel_im, rel_acc, lhs_rows, rhs_rows, rel_ids, neg_rows, bucket_step):
    info = jnp.stack([lax.axis_index("core"), lax.axis_index("x"), lax.axis_index("yl"), lax.axis_index("z")]).astype(I32)
    own = jnp.concatenate([ent_re, ent_im], 0)
    b1, b2, b3 = [shift(own, d) for d in (1, 2, 3)]
    neg = jnp.pad(neg_rows, ((0, 0), (0, 24)), constant_values=-1)
    head, relc, q, m, hit = call(
        query_kernel, "query", [(64, 256), (64, 256), (64, 256), (8, ROWS), (CH, ROWS)], [SM] + [VM] * 8,
    )(info, ent_re, ent_im, rel_re, rel_im, lhs_rows, rhs_rows, rel_ids, neg)
    quarter = (4, 32, ROWS)
    block = (2 * W, ROWS)
    keep, send = call(score_kernel, "score", [quarter, quarter], [SM, SM] + [VM] * 5)(info, bucket_step, q, own, b1, b2, b3)
    s = call(add_kernel, "add", quarter, [VM] * 2)(keep, lax.ppermute(send, "core", SWAP))
    s = exchange(s, "yl")
    w = call(weight_kernel, "weight", quarter, [SM, SM] + [VM] * 3)(info, bucket_step, s, m, hit)
    w_mine = exchange(w, "yl")
    w_other = lax.ppermute(w_mine, "core", SWAP)
    s0, s1, s2, s3, gr = call(
        grad_kernel, "grad", [block, block, block, block, (4, 2 * W + 1, 256)], [SM, SM] + [VM] * 11,
    )(info, bucket_step, q, head, relc, w_mine, w_other, own, b1, b2, b3, lhs_rows, rel_ids)
    got = [shift(s1, -1), shift(s2, -2), shift(s3, -3)]
    gr = exchange(gr, "x")
    pieces = call(place_kernel, "place", (8, 2 * W, 128), [SM, VM])(info, gr)
    half = call(fold_kernel, "fold", (2 * W, 128), [VM])(exchange(pieces, "z"))
    twin, got = lax.optimization_barrier((lax.ppermute(half, "yh", SWAP), got))
    rel, ent, sq = call(both_kernel, "both", [(32, 2 * W, 128), block, (8, 1, ROWS + 128)], [VM] * 6)(half, twin, s0, *got)
    rel = exchange(rel, ("x", "z"))
    new_re, new_im, new_acc, racc = call(
        entity_kernel, "entity", [(W, ROWS), (W, ROWS), (1, ROWS), (32, 1, 128)], [SM] + [VM] * 6
    )(info, exchange(sq, DIM), ent, ent_re, ent_im, ent_acc.reshape(1, ROWS), rel_acc.reshape(32, 128))
    new_rel_re, new_rel_im, new_rel_acc = call(
        relation_kernel, "relation", [(W, REL), (W, REL), (32, 128)], [VM] * 4
    )(rel, exchange(racc, ("x", "z")), rel_re, rel_im)
    return new_re, new_im, new_acc.reshape(ROWS), new_rel_re, new_rel_im, new_rel_acc.reshape(REL)


def solution(mesh):
    fine = Mesh(mesh.devices.reshape(2, 4, 8, 4, 2), DOM + DIM)
    return jax.shard_map(
        per_device,
        mesh=fine,
        in_specs=(
            P(DIM, DOM), P(DIM, DOM), P(DOM), P(DIM, None), P(DIM, None), P(),
            P(DOM, None), P(DOM, None), P(DOM, None), P(DOM, None), P(DOM),
        ),
        out_specs=(P(DIM, DOM), P(DIM, DOM), P(DOM), P(DIM, None), P(DIM, None), P()),
        check_vma=False,
    )
```

```python
import jax
import jax.numpy as jnp
from jax import lax
from jax.experimental import pallas as pl
from jax.experimental.pallas import tpu as pltpu
from jax.sharding import Mesh, PartitionSpec as P

D = 400
STEPS = 4
LEARN_RATE = 0.1
W = 25
ROWS = 512
CH = 128
REL = 4096
DOM = ("yh", "x", "z")
DIM = ("yl", "core")
SWAP = [(0, 1), (1, 0)]
F32 = jnp.float32
BF16 = jnp.bfloat16
I32 = jnp.int32
HIGHEST = lax.Precision.HIGHEST
VM = pl.BlockSpec(memory_space=pltpu.VMEM)
SM = pl.BlockSpec(memory_space=pltpu.SMEM)


def call(kernel, name, outs, specs):
    single = isinstance(outs, tuple)
    shapes = [jax.ShapeDtypeStruct(s, F32) for s in ([outs] if single else outs)]
    return pl.pallas_call(
        kernel,
        out_shape=shapes[0] if single else shapes,
        in_specs=specs,
        out_specs=VM if single else [VM] * len(shapes),
        compiler_params=pltpu.CompilerParams(vmem_limit_bytes=32 * 1024 * 1024),
        name=name,
    )


def iota(shape, axis):
    return lax.broadcasted_iota(I32, shape, axis)


def split3(x):
    hi = x.astype(BF16)
    rest = x - hi.astype(F32)
    mid = rest.astype(BF16)
    lo = (rest - mid.astype(F32)).astype(BF16)
    return jnp.concatenate([hi, mid, lo], 0)


def join3(y):
    r = y.shape[0] // 3
    return y[:r] + (y[r : 2 * r] + y[2 * r :])


def nn(a, b):
    return lax.dot_general(a, b, (((1,), (0,)), ((), ())), preferred_element_type=F32)


def nt(a, b):
    return lax.dot_general(a, b, (((1,), (1,)), ((), ())), preferred_element_type=F32)


def onehot_rows(ids, count):
    return jnp.where(iota((count, ids.shape[1]), 0) == ids, 1.0, 0.0).astype(BF16)


def pad32(x):
    return jnp.concatenate([x, jnp.zeros((32 - W, x.shape[1]), F32)], 0)


def pack(block):
    return jnp.concatenate([pad32(block[:W]), pad32(block[W:])], 0)


def edge_ids(ref):
    return jnp.concatenate([ref[0:1, :], ref[1:2, :]], 1)


def query_kernel(info, ent_re, ent_im, rel_re, rel_im, lhs, rhs, rel_ids, neg, head_o, relc_o, q_o, m_o, hit_o):
    own = jnp.concatenate([pad32(ent_re[...]), pad32(ent_im[...])], 0)
    head = join3(nn(split3(own), onehot_rows(edge_ids(lhs), ROWS)))
    ids = edge_ids(rel_ids)
    step = 1024
    acc = jnp.zeros((192, 2 * CH), F32)
    for k in range(0, REL, step):
        part = jnp.concatenate([pad32(rel_re[:, k : k + step]), pad32(rel_im[:, k : k + step])], 0)
        acc = acc + nn(split3(part), onehot_rows(ids - k, step))
    relc = join3(acc)
    head_o[...] = head
    relc_o[...] = relc
    h_re, h_im = head[:32], head[32:]
    r_re, r_im = relc[:32], relc[32:]
    q_o[...] = jnp.concatenate([h_re * r_re - h_im * r_im, h_re * r_im + h_im * r_re], 0)
    first = info[0] == 0
    ones = jnp.ones((16, neg.shape[1]), BF16)
    m_o[...] = nt(ones, onehot_rows(jnp.where(first, neg[0:1, :], neg[1:2, :]), ROWS))[:8]
    ids = jnp.where(first, rhs[0:1, :], rhs[1:2, :])
    hit_o[...] = jnp.transpose(jnp.where(iota((ROWS, CH), 0) == ids, 1.0, 0.0))


def choose(step, blocks):
    b = blocks[STEPS - 1]
    for s in range(STEPS - 1):
        b = jnp.where(step == s, blocks[s], b)
    return b


def score_kernel(info, bucket, q_r, b0, b1, b2, b3, keep_o, send_o):
    core = info[0]
    blocks = [pack(b[...]) for b in (b0, b1, b2, b3)]
    q = [q_r[:, 0:CH], q_r[:, CH : 2 * CH]]
    for first, out in ((1, send_o), (0, keep_o)):
        c = core ^ first
        s = lax.dot_general(
            jnp.where(c == 0, q[0], q[1]), choose(bucket[c], blocks),
            (((0,), (0,)), ((), ())), precision=HIGHEST, preferred_element_type=F32)
        for yl in range(4):
            out[yl] = s[32 * yl : 32 * yl + 32]


def add_kernel(a, b, o):
    o[...] = a[...] + b[...]


def weight_kernel(info, bucket, parts, m_r, hit_r, w_o):
    s = parts[0]
    for i in range(1, 4):
        s = s + parts[i]
    m = m_r[0:1, :]
    live = jnp.where(jnp.where(info[0] == 0, bucket[0], bucket[1]) < STEPS, 1.0, 0.0)
    hit = hit_r[pl.ds(pl.multiple_of(info[2] * 32, 32), 32), :] > 0.5
    pos = jnp.sum(jnp.where(hit, s, 0.0), 1, keepdims=True)
    masked = jnp.where(m > 0.0, s, -1e30)
    top = jnp.maximum(jnp.max(masked, 1, keepdims=True), pos)
    e_pos = jnp.exp(pos - top)
    e_neg = m * jnp.exp(masked - top)
    denom = e_pos + jnp.sum(e_neg, 1, keepdims=True)
    w_pos = (e_pos / denom - 1.0) * live
    w = e_neg * (live / denom) + jnp.where(hit, w_pos, 0.0)
    for i in range(4):
        w_o[i] = w


def grad_kernel(info, bucket, q_r, head_r, relc_r, w_mine, w_other, b0, b1, b2, b3, lhs, rel_ids, s0_o, s1_o, s2_o, s3_o, gr_o):
    core = info[0]
    mine = w_mine[...].reshape(CH, ROWS)
    other = w_other[...].reshape(CH, ROWS)
    blocks = [pack(b[...]) for b in (b0, b1, b2, b3)]
    gq = []
    slots = [jnp.zeros((64, ROWS), F32) for _ in range(STEPS)]
    for c in range(2):
        w = jnp.where(core == c, mine, other)
        step = jnp.minimum(bucket[c], STEPS - 1)
        block = choose(step, blocks)
        gq.append(lax.dot_general(block, w, (((1,), (1,)), ((), ())), precision=HIGHEST, preferred_element_type=F32))
        g = lax.dot_general(q_r[:, c * CH : (c + 1) * CH], w, (((1,), (0,)), ((), ())), precision=HIGHEST, preferred_element_type=F32)
        for s in range(STEPS):
            slots[s] = slots[s] + jnp.where(step == s, g, 0.0)
    gq = jnp.concatenate(gq, 1)
    g_re, g_im = gq[:32], gq[32:]
    h_re, h_im = head_r[:32, :], head_r[32:, :]
    r_re, r_im = relc_r[:32, :], relc_r[32:, :]
    gh = jnp.concatenate([g_re * r_re + g_im * r_im, g_im * r_re - g_re * r_im], 0)
    slots[0] = slots[0] + join3(nt(split3(gh), onehot_rows(edge_ids(lhs), ROWS)))
    gr_re = (g_re * h_re + g_im * h_im)[:W]
    gr_im = (g_im * h_re - g_re * h_im)[:W]
    ids = edge_ids(rel_ids).astype(F32)
    for i in range(8):
        gr_o[i, 0:W, :] = gr_re
        gr_o[i, W : 2 * W, :] = gr_im
        gr_o[i, 2 * W : 2 * W + 1, :] = ids
    for ref, slot in zip((s0_o, s1_o, s2_o, s3_o), slots):
        ref[0:W, :] = slot[:W]
        ref[W : 2 * W, :] = slot[32 : 32 + W]


def place_kernel(info, gr, out):
    x = info[1]
    vals = []
    cols = []
    for i in range(8):
        vals.append(split3(pack(gr[i, 0 : 2 * W, :])))
        ids = gr[i, 2 * W : 2 * W + 1, :].astype(I32)
        cols.append(jnp.where(jnp.right_shift(ids, 10) == x, jnp.bitwise_and(ids, 1023), -1))
    total = join3(nt(jnp.concatenate(vals, 1), onehot_rows(jnp.concatenate(cols, 1), 1024)))
    for z in range(8):
        out[z, 0:W, :] = total[:W, 128 * z : 128 * z + 128]
        out[z, W : 2 * W, :] = total[32 : 32 + W, 128 * z : 128 * z + 128]


def square_kernel(parts, s0, got1, got2, got3, tot_o, ent_o, sq_o):
    tot = parts[0]
    for i in range(1, 8):
        tot = tot + parts[i]
    tot_o[...] = tot
    ent = s0[...] + (got1[...] + (got2[...] + got3[...]))
    ent_o[...] = ent
    es = jnp.sum(ent * ent, 0, keepdims=True)
    rs = jnp.sum(tot * tot, 0, keepdims=True)
    for i in range(8):
        sq_o[i, :, 0:ROWS] = es
        sq_o[i, :, ROWS : ROWS + 128] = rs


def update_kernel(info, sq, tot, ent, ent_re, ent_im, eacc, rel_re, rel_im, racc, re_o, im_o, acc_o, rel_o):
    s = sq[0]
    for i in range(1, 8):
        s = s + sq[i]
    tile = info[1] * 8 + info[3]
    lane = pl.ds(pl.multiple_of(tile * 128, 128), 128)
    acc = racc[pl.ds(tile, 1), :] + s[:, ROWS:] / D
    scale = LEARN_RATE / jnp.sqrt(acc)
    new_re = rel_re[:, lane] - scale * tot[0:W, :]
    new_im = rel_im[:, lane] - scale * tot[W : 2 * W, :]
    for i in range(32):
        rel_o[i, 0:W, :] = new_re
        rel_o[i, W : 2 * W, :] = new_im
        rel_o[i, 2 * W : 2 * W + 1, :] = acc
    acc = eacc[...] + s[:, :ROWS] / D
    acc_o[...] = acc
    scale = LEARN_RATE / jnp.sqrt(acc)
    re_o[...] = ent_re[...] - scale * ent[0:W, :]
    im_o[...] = ent_im[...] - scale * ent[W : 2 * W, :]


def spread_kernel(rel, re_o, im_o, acc_o):
    for t in range(32):
        at = slice(128 * t, 128 * t + 128)
        re_o[:, at] = rel[t, 0:W, :]
        im_o[:, at] = rel[t, W : 2 * W, :]
        acc_o[t : t + 1, :] = rel[t, 2 * W : 2 * W + 1, :]


def shift(block, distance):
    return lax.ppermute(block, DOM, [(i, (i + distance) % 64) for i in range(64)])


def exchange(pieces, axes):
    return lax.all_to_all(pieces, axes, 0, 0)


def per_device(ent_re, ent_im, ent_acc, rel_re, rel_im, rel_acc, lhs_rows, rhs_rows, rel_ids, neg_rows, bucket_step):
    info = jnp.stack([lax.axis_index("core"), lax.axis_index("x"), lax.axis_index("yl"), lax.axis_index("z")]).astype(I32)
    own = jnp.concatenate([ent_re, ent_im], 0)
    b1, b2, b3 = [shift(own, d) for d in (1, 2, 3)]
    neg = jnp.pad(neg_rows, ((0, 0), (0, 24)), constant_values=-1)
    head, relc, q, m, hit = call(
        query_kernel, "query", [(64, 256), (64, 256), (64, 256), (8, ROWS), (CH, ROWS)], [SM] + [VM] * 8,
    )(info, ent_re, ent_im, rel_re, rel_im, lhs_rows, rhs_rows, rel_ids, neg)
    quarter = (4, 32, ROWS)
    block = (2 * W, ROWS)
    keep, send = call(score_kernel, "score", [quarter, quarter], [SM, SM] + [VM] * 5)(info, bucket_step, q, own, b1, b2, b3)
    s = call(add_kernel, "add", quarter, [VM] * 2)(keep, lax.ppermute(send, "core", SWAP))
    s = exchange(s, "yl")
    w = call(weight_kernel, "weight", quarter, [SM, SM] + [VM] * 3)(info, bucket_step, s, m, hit)
    w_mine = exchange(w, "yl")
    w_other = lax.ppermute(w_mine, "core", SWAP)
    s0, s1, s2, s3, gr = call(
        grad_kernel, "grad", [block, block, block, block, (8, 2 * W + 1, 256)], [SM, SM] + [VM] * 11,
    )(info, bucket_step, q, head, relc, w_mine, w_other, own, b1, b2, b3, lhs_rows, rel_ids)
    got1, got2, got3 = shift(s1, -1), shift(s2, -2), shift(s3, -3)
    gr = exchange(gr, ("yh", "x"))
    pieces = call(place_kernel, "place", (8, 2 * W, 128), [SM, VM])(info, gr)
    pieces, got1, got2 = lax.optimization_barrier((pieces, got1, got2))
    pieces = exchange(pieces, "z")
    tot, ent, sq = call(square_kernel, "square", [(2 * W, 128), block, (8, 1, ROWS + 128)], [VM] * 5)(pieces, s0, got1, got2, got3)
    sq = exchange(sq, DIM)
    new_re, new_im, new_acc, rel = call(
        update_kernel, "update", [(W, ROWS), (W, ROWS), (1, ROWS), (32, 2 * W + 1, 128)], [SM] + [VM] * 9
    )(info, sq, tot, ent, ent_re, ent_im, ent_acc.reshape(1, ROWS), rel_re, rel_im, rel_acc.reshape(32, 128))
    rel = exchange(rel, ("x", "z"))
    new_rel_re, new_rel_im, new_rel_acc = call(spread_kernel, "spread", [(W, REL), (W, REL), (32, 128)], [VM])(rel)
    return new_re, new_im, new_acc.reshape(ROWS), new_rel_re, new_rel_im, new_rel_acc.reshape(REL)


def solution(mesh):
    fine = Mesh(mesh.devices.reshape(2, 4, 8, 4, 2), DOM + DIM)
    return jax.shard_map(
        per_device,
        mesh=fine,
        in_specs=(
            P(DIM, DOM), P(DIM, DOM), P(DOM), P(DIM, None), P(DIM, None), P(),
            P(DOM, None), P(DOM, None), P(DOM, None), P(DOM, None), P(DOM),
        ),
        out_specs=(P(DIM, DOM), P(DIM, DOM), P(DOM), P(DIM, None), P(DIM, None), P()),
        check_vma=False,
    )
```

```python
import jax
import jax.numpy as jnp
from jax import lax
from jax.experimental import pallas as pl
from jax.experimental.pallas import tpu as pltpu
from jax.sharding import Mesh, PartitionSpec as P

D = 400
STEPS = 4
LEARN_RATE = 0.1
W = 25
ROWS = 512
CH = 128
REL = 4096
DOM = ("yh", "x", "z")
DIM = ("yl", "core")
SWAP = [(0, 1), (1, 0)]
F32 = jnp.float32
BF16 = jnp.bfloat16
I32 = jnp.int32
HIGHEST = lax.Precision.HIGHEST
VM = pl.BlockSpec(memory_space=pltpu.VMEM)
SM = pl.BlockSpec(memory_space=pltpu.SMEM)


def call(kernel, name, outs, specs):
    single = isinstance(outs, tuple)
    shapes = [jax.ShapeDtypeStruct(s, F32) for s in ([outs] if single else outs)]
    return pl.pallas_call(
        kernel,
        out_shape=shapes[0] if single else shapes,
        in_specs=specs,
        out_specs=VM if single else [VM] * len(shapes),
        compiler_params=pltpu.CompilerParams(vmem_limit_bytes=32 * 1024 * 1024),
        name=name,
    )


def iota(shape, axis):
    return lax.broadcasted_iota(I32, shape, axis)


def split3(x):
    hi = x.astype(BF16)
    rest = x - hi.astype(F32)
    mid = rest.astype(BF16)
    lo = (rest - mid.astype(F32)).astype(BF16)
    return jnp.concatenate([hi, mid, lo], 0)


def join3(y):
    r = y.shape[0] // 3
    return y[:r] + (y[r : 2 * r] + y[2 * r :])


def nn(a, b):
    return lax.dot_general(a, b, (((1,), (0,)), ((), ())), preferred_element_type=F32)


def nt(a, b):
    return lax.dot_general(a, b, (((1,), (1,)), ((), ())), preferred_element_type=F32)


def onehot_rows(ids, count):
    return jnp.where(iota((count, ids.shape[1]), 0) == ids, 1.0, 0.0).astype(BF16)


def pad32(x):
    return jnp.concatenate([x, jnp.zeros((32 - W, x.shape[1]), F32)], 0)


def pack(block):
    return jnp.concatenate([pad32(block[:W]), pad32(block[W:])], 0)


def edge_ids(ref):
    return jnp.concatenate([ref[0:1, :], ref[1:2, :]], 1)


def query_kernel(info, ent_re, ent_im, rel_re, rel_im, lhs, rhs, rel_ids, neg, head_o, relc_o, q_o, m_o, hit_o):
    own = jnp.concatenate([pad32(ent_re[...]), pad32(ent_im[...])], 0)
    head = join3(nn(split3(own), onehot_rows(edge_ids(lhs), ROWS)))
    ids = edge_ids(rel_ids)
    step = 1024
    acc = jnp.zeros((192, 2 * CH), F32)
    for k in range(0, REL, step):
        part = jnp.concatenate([pad32(rel_re[:, k : k + step]), pad32(rel_im[:, k : k + step])], 0)
        acc = acc + nn(split3(part), onehot_rows(ids - k, step))
    relc = join3(acc)
    head_o[...] = head
    relc_o[...] = relc
    h_re, h_im = head[:32], head[32:]
    r_re, r_im = relc[:32], relc[32:]
    q_o[...] = jnp.concatenate([h_re * r_re - h_im * r_im, h_re * r_im + h_im * r_re], 0)
    first = info[0] == 0
    ones = jnp.ones((16, neg.shape[1]), BF16)
    m_o[...] = nt(ones, onehot_rows(jnp.where(first, neg[0:1, :], neg[1:2, :]), ROWS))[:8]
    ids = jnp.where(first, rhs[0:1, :], rhs[1:2, :])
    hit_o[...] = jnp.transpose(jnp.where(iota((ROWS, CH), 0) == ids, 1.0, 0.0))


def choose(step, blocks):
    b = blocks[STEPS - 1]
    for s in range(STEPS - 1):
        b = jnp.where(step == s, blocks[s], b)
    return b


def score_kernel(info, bucket, q_r, b0, b1, b2, b3, keep_o, send_o):
    core = info[0]
    blocks = [pack(b[...]) for b in (b0, b1, b2, b3)]
    q = [q_r[:, 0:CH], q_r[:, CH : 2 * CH]]
    for first, out in ((1, send_o), (0, keep_o)):
        c = core ^ first
        s = lax.dot_general(
            jnp.where(c == 0, q[0], q[1]), choose(bucket[c], blocks),
            (((0,), (0,)), ((), ())), precision=HIGHEST, preferred_element_type=F32)
        for yl in range(4):
            out[yl] = s[32 * yl : 32 * yl + 32]


def add_kernel(a, b, o):
    o[...] = a[...] + b[...]


def weight_kernel(info, bucket, parts, m_r, hit_r, w_o):
    s = parts[0]
    for i in range(1, 4):
        s = s + parts[i]
    m = m_r[0:1, :]
    live = jnp.where(jnp.where(info[0] == 0, bucket[0], bucket[1]) < STEPS, 1.0, 0.0)
    hit = hit_r[pl.ds(pl.multiple_of(info[2] * 32, 32), 32), :] > 0.5
    pos = jnp.sum(jnp.where(hit, s, 0.0), 1, keepdims=True)
    masked = jnp.where(m > 0.0, s, -1e30)
    top = jnp.maximum(jnp.max(masked, 1, keepdims=True), pos)
    e_pos = jnp.exp(pos - top)
    e_neg = m * jnp.exp(masked - top)
    denom = e_pos + jnp.sum(e_neg, 1, keepdims=True)
    w_pos = (e_pos / denom - 1.0) * live
    w = e_neg * (live / denom) + jnp.where(hit, w_pos, 0.0)
    for i in range(4):
        w_o[i] = w


def grad_kernel(info, bucket, q_r, head_r, relc_r, w_mine, w_other, b0, b1, b2, b3, lhs, rel_ids, s0_o, s1_o, s23_o, gr_o):
    core = info[0]
    mine = w_mine[...].reshape(CH, ROWS)
    other = w_other[...].reshape(CH, ROWS)
    blocks = [pack(b[...]) for b in (b0, b1, b2, b3)]
    gq = []
    slots = [jnp.zeros((64, ROWS), F32) for _ in range(STEPS)]
    for c in range(2):
        w = jnp.where(core == c, mine, other)
        step = jnp.minimum(bucket[c], STEPS - 1)
        block = choose(step, blocks)
        gq.append(lax.dot_general(block, w, (((1,), (1,)), ((), ())), precision=HIGHEST, preferred_element_type=F32))
        g = lax.dot_general(q_r[:, c * CH : (c + 1) * CH], w, (((1,), (0,)), ((), ())), precision=HIGHEST, preferred_element_type=F32)
        for s in range(STEPS):
            slots[s] = slots[s] + jnp.where(step == s, g, 0.0)
    gq = jnp.concatenate(gq, 1)
    g_re, g_im = gq[:32], gq[32:]
    h_re, h_im = head_r[:32, :], head_r[32:, :]
    r_re, r_im = relc_r[:32, :], relc_r[32:, :]
    gh = jnp.concatenate([g_re * r_re + g_im * r_im, g_im * r_re - g_re * r_im], 0)
    slots[0] = slots[0] + join3(nt(split3(gh), onehot_rows(edge_ids(lhs), ROWS)))
    gr_re = (g_re * h_re + g_im * h_im)[:W]
    gr_im = (g_im * h_re - g_re * h_im)[:W]
    ids = edge_ids(rel_ids).astype(F32)
    for i in range(8):
        gr_o[i, 0:W, :] = gr_re
        gr_o[i, W : 2 * W, :] = gr_im
        gr_o[i, 2 * W : 2 * W + 1, :] = ids
    for ref, at, slot in ((s0_o, 0, 0), (s1_o, 0, 1), (s23_o, 0, 3), (s23_o, 2 * W, 2)):
        ref[at : at + W, :] = slots[slot][:W]
        ref[at + W : at + 2 * W, :] = slots[slot][32 : 32 + W]


def place_kernel(info, gr, out):
    x = info[1]
    vals = []
    cols = []
    for i in range(8):
        vals.append(split3(pack(gr[i, 0 : 2 * W, :])))
        ids = gr[i, 2 * W : 2 * W + 1, :].astype(I32)
        cols.append(jnp.where(jnp.right_shift(ids, 10) == x, jnp.bitwise_and(ids, 1023), -1))
    total = join3(nt(jnp.concatenate(vals, 1), onehot_rows(jnp.concatenate(cols, 1), 1024)))
    for z in range(8):
        out[z, 0:W, :] = total[:W, 128 * z : 128 * z + 128]
        out[z, W : 2 * W, :] = total[32 : 32 + W, 128 * z : 128 * z + 128]


def total_kernel(parts, out):
    tot = parts[0]
    for i in range(1, 8):
        tot = tot + parts[i]
    for i in range(32):
        out[i] = tot


def square_kernel(rel, s0, got1, got23, ent_o, sq_o):
    ent = s0[...] + (got1[...] + got23[2 * W : 4 * W, :])
    ent_o[...] = ent
    es = jnp.sum(ent * ent, 0, keepdims=True)
    for i in range(8):
        sq_o[i, :, 0:ROWS] = es
    for t in range(32):
        tot = rel[t]
        rs = jnp.sum(tot * tot, 0, keepdims=True)
        for i in range(8):
            sq_o[i, :, ROWS + 128 * t : ROWS + 128 * t + 128] = rs


def update_kernel(sq, rel, ent, ent_re, ent_im, eacc, rel_re, rel_im, racc, re_o, im_o, acc_o, rre_o, rim_o, racc_o):
    s = sq[0]
    for i in range(1, 8):
        s = s + sq[i]
    acc = eacc[...] + s[:, :ROWS] / D
    acc_o[...] = acc
    scale = LEARN_RATE / jnp.sqrt(acc)
    re_o[...] = ent_re[...] - scale * ent[0:W, :]
    im_o[...] = ent_im[...] - scale * ent[W : 2 * W, :]
    acc = racc[...] + s[:, ROWS:] / D
    racc_o[...] = acc
    scale = LEARN_RATE / jnp.sqrt(acc)
    for t in range(32):
        at = slice(128 * t, 128 * t + 128)
        tot = rel[t]
        rre_o[:, at] = rel_re[:, at] - scale[:, at] * tot[:W]
        rim_o[:, at] = rel_im[:, at] - scale[:, at] * tot[W:]


def shift(block, distance):
    return lax.ppermute(block, DOM, [(i, (i + distance) % 64) for i in range(64)])


def exchange(pieces, axes):
    return lax.all_to_all(pieces, axes, 0, 0)


def per_device(ent_re, ent_im, ent_acc, rel_re, rel_im, rel_acc, lhs_rows, rhs_rows, rel_ids, neg_rows, bucket_step):
    info = jnp.stack([lax.axis_index("core"), lax.axis_index("x"), lax.axis_index("yl")]).astype(I32)
    own = jnp.concatenate([ent_re, ent_im], 0)
    b1, b2, b3 = [shift(own, d) for d in (1, 2, 3)]
    neg = jnp.pad(neg_rows, ((0, 0), (0, 24)), constant_values=-1)
    head, relc, q, m, hit = call(
        query_kernel, "query", [(64, 256), (64, 256), (64, 256), (8, ROWS), (CH, ROWS)], [SM] + [VM] * 8,
    )(info, ent_re, ent_im, rel_re, rel_im, lhs_rows, rhs_rows, rel_ids, neg)
    quarter = (4, 32, ROWS)
    block = (2 * W, ROWS)
    keep, send = call(score_kernel, "score", [quarter, quarter], [SM, SM] + [VM] * 5)(info, bucket_step, q, own, b1, b2, b3)
    s = call(add_kernel, "add", quarter, [VM] * 2)(keep, lax.ppermute(send, "core", SWAP))
    s = exchange(s, "yl")
    w = call(weight_kernel, "weight", quarter, [SM, SM] + [VM] * 3)(info, bucket_step, s, m, hit)
    w_mine = exchange(w, "yl")
    w_other = lax.ppermute(w_mine, "core", SWAP)
    s0, s1, s23, gr = call(
        grad_kernel, "grad", [block, block, (4 * W, ROWS), (8, 2 * W + 1, 256)], [SM, SM] + [VM] * 11,
    )(info, bucket_step, q, head, relc, w_mine, w_other, own, b1, b2, b3, lhs_rows, rel_ids)
    got23 = shift(s23, -2)
    gr = exchange(gr, ("yh", "x"))
    pieces = call(place_kernel, "place", (8, 2 * W, 128), [SM, VM])(info, gr)
    pieces, got23 = lax.optimization_barrier((pieces, got23))
    got1 = shift(s1 + got23[: 2 * W], -1)
    rel = call(total_kernel, "total", (32, 2 * W, 128), [VM])(exchange(pieces, "z"))
    rel = exchange(rel, ("x", "z"))
    ent, sq = call(square_kernel, "square", [block, (8, 1, ROWS + REL)], [VM] * 4)(rel, s0, got1, got23)
    sq = exchange(sq, DIM)
    new_re, new_im, new_acc, new_rel_re, new_rel_im, new_rel_acc = call(
        update_kernel, "update", [(W, ROWS), (W, ROWS), (1, ROWS), (W, REL), (W, REL), (1, REL)], [VM] * 9
    )(sq, rel, ent, ent_re, ent_im, ent_acc.reshape(1, ROWS), rel_re, rel_im, rel_acc.reshape(1, REL))
    return new_re, new_im, new_acc.reshape(ROWS), new_rel_re, new_rel_im, new_rel_acc.reshape(REL)


def solution(mesh):
    fine = Mesh(mesh.devices.reshape(2, 4, 8, 4, 2), DOM + DIM)
    return jax.shard_map(
        per_device,
        mesh=fine,
        in_specs=(
            P(DIM, DOM), P(DIM, DOM), P(DOM), P(DIM, None), P(DIM, None), P(),
            P(DOM, None), P(DOM, None), P(DOM, None), P(DOM, None), P(DOM),
        ),
        out_specs=(P(DIM, DOM), P(DIM, DOM), P(DOM), P(DIM, None), P(DIM, None), P()),
        check_vma=False,
    )
```

```python
import jax
import jax.numpy as jnp
from jax import lax
from jax.experimental import pallas as pl
from jax.experimental.pallas import tpu as pltpu
from jax.sharding import Mesh, PartitionSpec as P

D = 400
STEPS = 4
LEARN_RATE = 0.1
W = 25
ROWS = 512
CH = 128
REL = 4096
DOM = ("yh", "x", "z")
DIM = ("yl", "core")
SWAP = [(0, 1), (1, 0)]
F32 = jnp.float32
BF16 = jnp.bfloat16
I32 = jnp.int32
HIGHEST = lax.Precision.HIGHEST
VM = pl.BlockSpec(memory_space=pltpu.VMEM)
SM = pl.BlockSpec(memory_space=pltpu.SMEM)


def call(kernel, name, outs, specs):
    single = isinstance(outs, tuple)
    shapes = [jax.ShapeDtypeStruct(s, F32) for s in ([outs] if single else outs)]
    return pl.pallas_call(
        kernel,
        out_shape=shapes[0] if single else shapes,
        in_specs=specs,
        out_specs=VM if single else [VM] * len(shapes),
        compiler_params=pltpu.CompilerParams(vmem_limit_bytes=32 * 1024 * 1024),
        name=name,
    )


def iota(shape, axis):
    return lax.broadcasted_iota(I32, shape, axis)


def split3(x):
    hi = x.astype(BF16)
    rest = x - hi.astype(F32)
    mid = rest.astype(BF16)
    lo = (rest - mid.astype(F32)).astype(BF16)
    return jnp.concatenate([hi, mid, lo], 0)


def join3(y):
    r = y.shape[0] // 3
    return y[:r] + (y[r : 2 * r] + y[2 * r :])


def nn(a, b):
    return lax.dot_general(a, b, (((1,), (0,)), ((), ())), preferred_element_type=F32)


def nt(a, b):
    return lax.dot_general(a, b, (((1,), (1,)), ((), ())), preferred_element_type=F32)


def onehot_rows(ids, count):
    return jnp.where(iota((count, ids.shape[1]), 0) == ids, 1.0, 0.0).astype(BF16)


def pad32(x):
    return jnp.concatenate([x, jnp.zeros((32 - W, x.shape[1]), F32)], 0)


def pack(block):
    return jnp.concatenate([pad32(block[:W]), pad32(block[W:])], 0)


def edge_ids(ref):
    return jnp.concatenate([ref[0:1, :], ref[1:2, :]], 1)


def query_kernel(info, ent_re, ent_im, rel_re, rel_im, lhs, rhs, rel_ids, neg, head_o, relc_o, q_o, m_o, hit_o):
    own = jnp.concatenate([pad32(ent_re[...]), pad32(ent_im[...])], 0)
    head = join3(nn(split3(own), onehot_rows(edge_ids(lhs), ROWS)))
    ids = edge_ids(rel_ids)
    step = 1024
    acc = jnp.zeros((192, 2 * CH), F32)
    for k in range(0, REL, step):
        part = jnp.concatenate([pad32(rel_re[:, k : k + step]), pad32(rel_im[:, k : k + step])], 0)
        acc = acc + nn(split3(part), onehot_rows(ids - k, step))
    relc = join3(acc)
    head_o[...] = head
    relc_o[...] = relc
    h_re, h_im = head[:32], head[32:]
    r_re, r_im = relc[:32], relc[32:]
    q_o[...] = jnp.concatenate([h_re * r_re - h_im * r_im, h_re * r_im + h_im * r_re], 0)
    first = info[0] == 0
    ones = jnp.ones((16, neg.shape[1]), BF16)
    m_o[...] = nt(ones, onehot_rows(jnp.where(first, neg[0:1, :], neg[1:2, :]), ROWS))[:8]
    ids = jnp.where(first, rhs[0:1, :], rhs[1:2, :])
    hit_o[...] = jnp.transpose(jnp.where(iota((ROWS, CH), 0) == ids, 1.0, 0.0))


def choose(step, blocks):
    b = blocks[STEPS - 1]
    for s in range(STEPS - 1):
        b = jnp.where(step == s, blocks[s], b)
    return b


def score_kernel(info, bucket, q_r, b0, b1, b2, b3, keep_o, send_o):
    core = info[0]
    blocks = [pack(b[...]) for b in (b0, b1, b2, b3)]
    q = [q_r[:, 0:CH], q_r[:, CH : 2 * CH]]
    for first, out in ((1, send_o), (0, keep_o)):
        c = core ^ first
        s = lax.dot_general(
            jnp.where(c == 0, q[0], q[1]), choose(bucket[c], blocks),
            (((0,), (0,)), ((), ())), precision=HIGHEST, preferred_element_type=F32)
        for yl in range(4):
            out[yl] = s[32 * yl : 32 * yl + 32]


def add_kernel(a, b, o):
    o[...] = a[...] + b[...]


def weight_kernel(info, bucket, parts, m_r, hit_r, w_o):
    s = parts[0]
    for i in range(1, 4):
        s = s + parts[i]
    m = m_r[0:1, :]
    live = jnp.where(jnp.where(info[0] == 0, bucket[0], bucket[1]) < STEPS, 1.0, 0.0)
    hit = hit_r[pl.ds(pl.multiple_of(info[2] * 32, 32), 32), :] > 0.5
    pos = jnp.sum(jnp.where(hit, s, 0.0), 1, keepdims=True)
    masked = jnp.where(m > 0.0, s, -1e30)
    top = jnp.maximum(jnp.max(masked, 1, keepdims=True), pos)
    e_pos = jnp.exp(pos - top)
    e_neg = m * jnp.exp(masked - top)
    denom = e_pos + jnp.sum(e_neg, 1, keepdims=True)
    w_pos = (e_pos / denom - 1.0) * live
    w = e_neg * (live / denom) + jnp.where(hit, w_pos, 0.0)
    for i in range(4):
        w_o[i] = w


def grad_kernel(info, bucket, q_r, head_r, relc_r, w_mine, w_other, b0, b1, b2, b3, lhs, rel_ids, s0_o, s1_o, s2_o, s3_o, gr_o):
    core = info[0]
    mine = w_mine[...].reshape(CH, ROWS)
    other = w_other[...].reshape(CH, ROWS)
    blocks = [pack(b[...]) for b in (b0, b1, b2, b3)]
    gq = []
    slots = [jnp.zeros((64, ROWS), F32) for _ in range(STEPS)]
    for c in range(2):
        w = jnp.where(core == c, mine, other)
        step = jnp.minimum(bucket[c], STEPS - 1)
        block = choose(step, blocks)
        gq.append(lax.dot_general(block, w, (((1,), (1,)), ((), ())), precision=HIGHEST, preferred_element_type=F32))
        g = lax.dot_general(q_r[:, c * CH : (c + 1) * CH], w, (((1,), (0,)), ((), ())), precision=HIGHEST, preferred_element_type=F32)
        for s in range(STEPS):
            slots[s] = slots[s] + jnp.where(step == s, g, 0.0)
    gq = jnp.concatenate(gq, 1)
    g_re, g_im = gq[:32], gq[32:]
    h_re, h_im = head_r[:32, :], head_r[32:, :]
    r_re, r_im = relc_r[:32, :], relc_r[32:, :]
    gh = jnp.concatenate([g_re * r_re + g_im * r_im, g_im * r_re - g_re * r_im], 0)
    slots[0] = slots[0] + join3(nt(split3(gh), onehot_rows(edge_ids(lhs), ROWS)))
    gr_re = (g_re * h_re + g_im * h_im)[:W]
    gr_im = (g_im * h_re - g_re * h_im)[:W]
    ids = edge_ids(rel_ids).astype(F32)
    for i in range(4):
        gr_o[i, 0:W, :] = gr_re
        gr_o[i, W : 2 * W, :] = gr_im
        gr_o[i, 2 * W : 2 * W + 1, :] = ids
    for ref, slot in zip((s0_o, s1_o, s2_o, s3_o), slots):
        ref[0:W, :] = slot[:W]
        ref[W : 2 * W, :] = slot[32 : 32 + W]


def place_kernel(info, gr, out):
    x = info[1]
    vals = []
    cols = []
    for i in range(4):
        vals.append(split3(pack(gr[i, 0 : 2 * W, :])))
        ids = gr[i, 2 * W : 2 * W + 1, :].astype(I32)
        cols.append(jnp.where(jnp.right_shift(ids, 10) == x, jnp.bitwise_and(ids, 1023), -1))
    total = join3(nt(jnp.concatenate(vals, 1), onehot_rows(jnp.concatenate(cols, 1), 1024)))
    for z in range(8):
        out[z, 0:W, :] = total[:W, 128 * z : 128 * z + 128]
        out[z, W : 2 * W, :] = total[32 : 32 + W, 128 * z : 128 * z + 128]


def fold_kernel(parts, out):
    tot = parts[0]
    for i in range(1, 8):
        tot = tot + parts[i]
    out[...] = tot


def both_kernel(info, a, b, s0, got1, got2, got3, out, ring_o, wrap_o):
    tot = a[...] + b[...]
    for i in range(32):
        out[i] = tot
    z = info[3]
    ring = s0[...]
    wrap = jnp.zeros_like(ring)
    for s, got in ((1, got1), (2, got2), (3, got3)):
        ring = ring + jnp.where(z + s < 8, got[...], 0.0)
        wrap = wrap + jnp.where(z + s < 8, 0.0, got[...])
    ring_o[...] = ring
    wrap_o[...] = wrap


def square_kernel(rel, ring, wrap, ent_o, sq_o):
    ent = ring[...] + wrap[...]
    ent_o[...] = ent
    es = jnp.sum(ent * ent, 0, keepdims=True)
    for i in range(8):
        sq_o[i, :, 0:ROWS] = es
    for t in range(32):
        tot = rel[t]
        rs = jnp.sum(tot * tot, 0, keepdims=True)
        for i in range(8):
            sq_o[i, :, ROWS + 128 * t : ROWS + 128 * t + 128] = rs


def update_kernel(sq, rel, ent, ent_re, ent_im, eacc, rel_re, rel_im, racc, re_o, im_o, acc_o, rre_o, rim_o, racc_o):
    s = sq[0]
    for i in range(1, 8):
        s = s + sq[i]
    acc = eacc[...] + s[:, :ROWS] / D
    acc_o[...] = acc
    scale = LEARN_RATE / jnp.sqrt(acc)
    re_o[...] = ent_re[...] - scale * ent[0:W, :]
    im_o[...] = ent_im[...] - scale * ent[W : 2 * W, :]
    acc = racc[...] + s[:, ROWS:] / D
    racc_o[...] = acc
    scale = LEARN_RATE / jnp.sqrt(acc)
    for t in range(32):
        at = slice(128 * t, 128 * t + 128)
        tot = rel[t]
        rre_o[:, at] = rel_re[:, at] - scale[:, at] * tot[:W]
        rim_o[:, at] = rel_im[:, at] - scale[:, at] * tot[W:]


def shift(block, distance):
    return lax.ppermute(block, DOM, [(i, (i + distance) % 64) for i in range(64)])


def exchange(pieces, axes):
    return lax.all_to_all(pieces, axes, 0, 0)


def per_device(ent_re, ent_im, ent_acc, rel_re, rel_im, rel_acc, lhs_rows, rhs_rows, rel_ids, neg_rows, bucket_step):
    info = jnp.stack([lax.axis_index("core"), lax.axis_index("x"), lax.axis_index("yl"), lax.axis_index("z")]).astype(I32)
    own = jnp.concatenate([ent_re, ent_im], 0)
    b1, b2, b3 = [shift(own, d) for d in (1, 2, 3)]
    neg = jnp.pad(neg_rows, ((0, 0), (0, 24)), constant_values=-1)
    head, relc, q, m, hit = call(
        query_kernel, "query", [(64, 256), (64, 256), (64, 256), (8, ROWS), (CH, ROWS)], [SM] + [VM] * 8,
    )(info, ent_re, ent_im, rel_re, rel_im, lhs_rows, rhs_rows, rel_ids, neg)
    quarter = (4, 32, ROWS)
    block = (2 * W, ROWS)
    keep, send = call(score_kernel, "score", [quarter, quarter], [SM, SM] + [VM] * 5)(info, bucket_step, q, own, b1, b2, b3)
    s = call(add_kernel, "add", quarter, [VM] * 2)(keep, lax.ppermute(send, "core", SWAP))
    s = exchange(s, "yl")
    w = call(weight_kernel, "weight", quarter, [SM, SM] + [VM] * 3)(info, bucket_step, s, m, hit)
    w_mine = exchange(w, "yl")
    w_other = lax.ppermute(w_mine, "core", SWAP)
    s0, s1, s2, s3, gr = call(
        grad_kernel, "grad", [block, block, block, block, (4, 2 * W + 1, 256)], [SM, SM] + [VM] * 11,
    )(info, bucket_step, q, head, relc, w_mine, w_other, own, b1, b2, b3, lhs_rows, rel_ids)
    got = [lax.ppermute(v, "z", [(i, (i - d) % 8) for i in range(8)]) for d, v in ((1, s1), (2, s2), (3, s3))]
    gr = exchange(gr, "x")
    pieces = call(place_kernel, "place", (8, 2 * W, 128), [SM, VM])(info, gr)
    half = call(fold_kernel, "fold", (2 * W, 128), [VM])(exchange(pieces, "z"))
    twin, got = lax.optimization_barrier((lax.ppermute(half, "yh", SWAP), got))
    rel, ring, wrap = call(both_kernel, "both", [(32, 2 * W, 128), block, block], [SM] + [VM] * 6)(info, half, twin, s0, *got)
    wrap = lax.ppermute(wrap, DOM, [(i, (i - 8) % 64) for i in range(64) if i % 8 >= 5])
    rel = exchange(rel, ("x", "z"))
    ent, sq = call(square_kernel, "square", [block, (8, 1, ROWS + REL)], [VM] * 3)(rel, ring, wrap)
    sq = exchange(sq, DIM)
    new_re, new_im, new_acc, new_rel_re, new_rel_im, new_rel_acc = call(
        update_kernel, "update", [(W, ROWS), (W, ROWS), (1, ROWS), (W, REL), (W, REL), (1, REL)], [VM] * 9
    )(sq, rel, ent, ent_re, ent_im, ent_acc.reshape(1, ROWS), rel_re, rel_im, rel_acc.reshape(1, REL))
    return new_re, new_im, new_acc.reshape(ROWS), new_rel_re, new_rel_im, new_rel_acc.reshape(REL)


def solution(mesh):
    fine = Mesh(mesh.devices.reshape(2, 4, 8, 4, 2), DOM + DIM)
    return jax.shard_map(
        per_device,
        mesh=fine,
        in_specs=(
            P(DIM, DOM), P(DIM, DOM), P(DOM), P(DIM, None), P(DIM, None), P(),
            P(DOM, None), P(DOM, None), P(DOM, None), P(DOM, None), P(DOM),
        ),
        out_specs=(P(DIM, DOM), P(DIM, DOM), P(DOM), P(DIM, None), P(DIM, None), P()),
        check_vma=False,
    )
```

```python
import jax
import jax.numpy as jnp
from jax import lax
from jax.experimental import pallas as pl
from jax.experimental.pallas import tpu as pltpu
from jax.sharding import Mesh, PartitionSpec as P

D = 400
STEPS = 4
LEARN_RATE = 0.1
W = 25
ROWS = 512
CH = 128
REL = 4096
DOM = ("yh", "x", "z")
DIM = ("yl", "core")
SWAP = [(0, 1), (1, 0)]
F32 = jnp.float32
BF16 = jnp.bfloat16
I32 = jnp.int32
HIGHEST = lax.Precision.HIGHEST
VM = pl.BlockSpec(memory_space=pltpu.VMEM)
SM = pl.BlockSpec(memory_space=pltpu.SMEM)


def call(kernel, name, outs, specs):
    single = isinstance(outs, tuple)
    shapes = [jax.ShapeDtypeStruct(s, F32) for s in ([outs] if single else outs)]
    return pl.pallas_call(
        kernel,
        out_shape=shapes[0] if single else shapes,
        in_specs=specs,
        out_specs=VM if single else [VM] * len(shapes),
        compiler_params=pltpu.CompilerParams(vmem_limit_bytes=32 * 1024 * 1024),
        name=name,
    )


def iota(shape, axis):
    return lax.broadcasted_iota(I32, shape, axis)


def split3(x):
    hi = x.astype(BF16)
    rest = x - hi.astype(F32)
    mid = rest.astype(BF16)
    lo = (rest - mid.astype(F32)).astype(BF16)
    return jnp.concatenate([hi, mid, lo], 0)


def join3(y):
    r = y.shape[0] // 3
    return y[:r] + (y[r : 2 * r] + y[2 * r :])


def nn(a, b):
    return lax.dot_general(a, b, (((1,), (0,)), ((), ())), preferred_element_type=F32)


def nt(a, b):
    return lax.dot_general(a, b, (((1,), (1,)), ((), ())), preferred_element_type=F32)


def onehot_rows(ids, count):
    return jnp.where(iota((count, ids.shape[1]), 0) == ids, 1.0, 0.0).astype(BF16)


def pad32(x):
    return jnp.concatenate([x, jnp.zeros((32 - W, x.shape[1]), F32)], 0)


def pack(block):
    return jnp.concatenate([pad32(block[:W]), pad32(block[W:])], 0)


def edge_ids(ref):
    return jnp.concatenate([ref[0:1, :], ref[1:2, :]], 1)


def query_kernel(info, ent_re, ent_im, rel_re, rel_im, lhs, rhs, rel_ids, neg, head_o, relc_o, q_o, m_o, hit_o):
    own = jnp.concatenate([pad32(ent_re[...]), pad32(ent_im[...])], 0)
    head = join3(nn(split3(own), onehot_rows(edge_ids(lhs), ROWS)))
    ids = edge_ids(rel_ids)
    step = 1024
    acc = jnp.zeros((192, 2 * CH), F32)
    for k in range(0, REL, step):
        part = jnp.concatenate([pad32(rel_re[:, k : k + step]), pad32(rel_im[:, k : k + step])], 0)
        acc = acc + nn(split3(part), onehot_rows(ids - k, step))
    relc = join3(acc)
    head_o[...] = head
    relc_o[...] = relc
    h_re, h_im = head[:32], head[32:]
    r_re, r_im = relc[:32], relc[32:]
    q_o[...] = jnp.concatenate([h_re * r_re - h_im * r_im, h_re * r_im + h_im * r_re], 0)
    first = info[0] == 0
    ones = jnp.ones((16, neg.shape[1]), BF16)
    m_o[...] = nt(ones, onehot_rows(jnp.where(first, neg[0:1, :], neg[1:2, :]), ROWS))[:8]
    ids = jnp.where(first, rhs[0:1, :], rhs[1:2, :])
    hit_o[...] = jnp.transpose(jnp.where(iota((ROWS, CH), 0) == ids, 1.0, 0.0))


def choose(step, blocks):
    b = blocks[STEPS - 1]
    for s in range(STEPS - 1):
        b = jnp.where(step == s, blocks[s], b)
    return b


def score_kernel(info, bucket, q_r, b0, b1, b2, b3, keep_o, send_o):
    core = info[0]
    blocks = [pack(b[...]) for b in (b0, b1, b2, b3)]
    q = [q_r[:, 0:CH], q_r[:, CH : 2 * CH]]
    for first, out in ((1, send_o), (0, keep_o)):
        c = core ^ first
        s = lax.dot_general(
            jnp.where(c == 0, q[0], q[1]), choose(bucket[c], blocks),
            (((0,), (0,)), ((), ())), precision=HIGHEST, preferred_element_type=F32)
        for yl in range(4):
            out[yl] = s[32 * yl : 32 * yl + 32]


def add_kernel(a, b, o):
    o[...] = a[...] + b[...]


def weight_kernel(info, bucket, parts, m_r, hit_r, w_o):
    s = parts[0]
    for i in range(1, 4):
        s = s + parts[i]
    m = m_r[0:1, :]
    live = jnp.where(jnp.where(info[0] == 0, bucket[0], bucket[1]) < STEPS, 1.0, 0.0)
    hit = hit_r[pl.ds(pl.multiple_of(info[2] * 32, 32), 32), :] > 0.5
    pos = jnp.sum(jnp.where(hit, s, 0.0), 1, keepdims=True)
    masked = jnp.where(m > 0.0, s, -1e30)
    top = jnp.maximum(jnp.max(masked, 1, keepdims=True), pos)
    e_pos = jnp.exp(pos - top)
    e_neg = m * jnp.exp(masked - top)
    denom = e_pos + jnp.sum(e_neg, 1, keepdims=True)
    w_pos = (e_pos / denom - 1.0) * live
    w = e_neg * (live / denom) + jnp.where(hit, w_pos, 0.0)
    for i in range(4):
        w_o[i] = w


def grad_kernel(info, bucket, q_r, head_r, relc_r, w_mine, w_other, b0, b1, b2, b3, lhs, rel_ids, s0_o, s1_o, s23_o, gr_o):
    core = info[0]
    mine = w_mine[...].reshape(CH, ROWS)
    other = w_other[...].reshape(CH, ROWS)
    blocks = [pack(b[...]) for b in (b0, b1, b2, b3)]
    gq = []
    slots = [jnp.zeros((64, ROWS), F32) for _ in range(STEPS)]
    for c in range(2):
        w = jnp.where(core == c, mine, other)
        step = jnp.minimum(bucket[c], STEPS - 1)
        block = choose(step, blocks)
        gq.append(lax.dot_general(block, w, (((1,), (1,)), ((), ())), precision=HIGHEST, preferred_element_type=F32))
        g = lax.dot_general(q_r[:, c * CH : (c + 1) * CH], w, (((1,), (0,)), ((), ())), precision=HIGHEST, preferred_element_type=F32)
        for s in range(STEPS):
            slots[s] = slots[s] + jnp.where(step == s, g, 0.0)
    gq = jnp.concatenate(gq, 1)
    g_re, g_im = gq[:32], gq[32:]
    h_re, h_im = head_r[:32, :], head_r[32:, :]
    r_re, r_im = relc_r[:32, :], relc_r[32:, :]
    gh = jnp.concatenate([g_re * r_re + g_im * r_im, g_im * r_re - g_re * r_im], 0)
    slots[0] = slots[0] + join3(nt(split3(gh), onehot_rows(edge_ids(lhs), ROWS)))
    gr_re = (g_re * h_re + g_im * h_im)[:W]
    gr_im = (g_im * h_re - g_re * h_im)[:W]
    ids = edge_ids(rel_ids).astype(F32)
    for i in range(4):
        gr_o[i, 0:W, :] = gr_re
        gr_o[i, W : 2 * W, :] = gr_im
        gr_o[i, 2 * W : 2 * W + 1, :] = ids
    for ref, at, slot in ((s0_o, 0, 0), (s1_o, 0, 1), (s23_o, 0, 3), (s23_o, 2 * W, 2)):
        ref[at : at + W, :] = slots[slot][:W]
        ref[at + W : at + 2 * W, :] = slots[slot][32 : 32 + W]


def place_kernel(info, gr, out):
    x = info[1]
    vals = []
    cols = []
    for i in range(4):
        vals.append(split3(pack(gr[i, 0 : 2 * W, :])))
        ids = gr[i, 2 * W : 2 * W + 1, :].astype(I32)
        cols.append(jnp.where(jnp.right_shift(ids, 10) == x, jnp.bitwise_and(ids, 1023), -1))
    total = join3(nt(jnp.concatenate(vals, 1), onehot_rows(jnp.concatenate(cols, 1), 1024)))
    for z in range(8):
        out[z, 0:W, :] = total[:W, 128 * z : 128 * z + 128]
        out[z, W : 2 * W, :] = total[32 : 32 + W, 128 * z : 128 * z + 128]


def fold_kernel(parts, out):
    tot = parts[0]
    for i in range(1, 8):
        tot = tot + parts[i]
    out[...] = tot


def carry_kernel(info, s1, got23, out):
    z = info[3]
    own = s1[...]
    far = got23[0 : 2 * W, :]
    wraps = (z >= 6) | (z == 0)
    out[0 : 2 * W, :] = jnp.where(z == 0, 0.0, own) + jnp.where(wraps, 0.0, far)
    out[2 * W : 4 * W, :] = jnp.where(z == 0, own, 0.0) + jnp.where(wraps, far, 0.0)


def both_kernel(info, a, b, s0, got1, got23, out, ring_o, wrap_o):
    tot = a[...] + b[...]
    for i in range(8):
        out[i] = tot
    wraps = info[3] >= 6
    second = got23[2 * W : 4 * W, :]
    ring_o[...] = s0[...] + (got1[0 : 2 * W, :] + jnp.where(wraps, 0.0, second))
    wrap_o[...] = got1[2 * W : 4 * W, :] + jnp.where(wraps, second, 0.0)


def copies_kernel(a, out):
    for x in range(4):
        for z in range(8):
            out[x, 2 * W * z : 2 * W * z + 2 * W, :] = a[z]


def square_kernel(rel, ring, wrap, ent_o, sq_o):
    ent = ring[...] + wrap[...]
    ent_o[...] = ent
    es = jnp.sum(ent * ent, 0, keepdims=True)
    for i in range(8):
        sq_o[i, :, 0:ROWS] = es
    for t in range(32):
        tot = rel[t // 8, 2 * W * (t % 8) : 2 * W * (t % 8) + 2 * W, :]
        rs = jnp.sum(tot * tot, 0, keepdims=True)
        for i in range(8):
            sq_o[i, :, ROWS + 128 * t : ROWS + 128 * t + 128] = rs


def update_kernel(sq, rel, ent, ent_re, ent_im, eacc, rel_re, rel_im, racc, re_o, im_o, acc_o, rre_o, rim_o, racc_o):
    s = sq[0]
    for i in range(1, 8):
        s = s + sq[i]
    acc = eacc[...] + s[:, :ROWS] / D
    acc_o[...] = acc
    scale = LEARN_RATE / jnp.sqrt(acc)
    re_o[...] = ent_re[...] - scale * ent[0:W, :]
    im_o[...] = ent_im[...] - scale * ent[W : 2 * W, :]
    acc = racc[...] + s[:, ROWS:] / D
    racc_o[...] = acc
    scale = LEARN_RATE / jnp.sqrt(acc)
    for t in range(32):
        at = slice(128 * t, 128 * t + 128)
        tot = rel[t // 8, 2 * W * (t % 8) : 2 * W * (t % 8) + 2 * W, :]
        rre_o[:, at] = rel_re[:, at] - scale[:, at] * tot[:W]
        rim_o[:, at] = rel_im[:, at] - scale[:, at] * tot[W:]


def shift(block, distance):
    return lax.ppermute(block, DOM, [(i, (i + distance) % 64) for i in range(64)])


def exchange(pieces, axes):
    return lax.all_to_all(pieces, axes, 0, 0)


def per_device(ent_re, ent_im, ent_acc, rel_re, rel_im, rel_acc, lhs_rows, rhs_rows, rel_ids, neg_rows, bucket_step):
    info = jnp.stack([lax.axis_index("core"), lax.axis_index("x"), lax.axis_index("yl"), lax.axis_index("z")]).astype(I32)
    own = jnp.concatenate([ent_re, ent_im], 0)
    b1, b2, b3 = [shift(own, d) for d in (1, 2, 3)]
    neg = jnp.pad(neg_rows, ((0, 0), (0, 24)), constant_values=-1)
    head, relc, q, m, hit = call(
        query_kernel, "query", [(64, 256), (64, 256), (64, 256), (8, ROWS), (CH, ROWS)], [SM] + [VM] * 8,
    )(info, ent_re, ent_im, rel_re, rel_im, lhs_rows, rhs_rows, rel_ids, neg)
    quarter = (4, 32, ROWS)
    block = (2 * W, ROWS)
    keep, send = call(score_kernel, "score", [quarter, quarter], [SM, SM] + [VM] * 5)(info, bucket_step, q, own, b1, b2, b3)
    s = call(add_kernel, "add", quarter, [VM] * 2)(keep, lax.ppermute(send, "core", SWAP))
    s = exchange(s, "yl")
    w = call(weight_kernel, "weight", quarter, [SM, SM] + [VM] * 3)(info, bucket_step, s, m, hit)
    w_mine = exchange(w, "yl")
    w_other = lax.ppermute(w_mine, "core", SWAP)
    s0, s1, s23, gr = call(
        grad_kernel, "grad", [block, block, (4 * W, ROWS), (4, 2 * W + 1, 256)], [SM, SM] + [VM] * 11,
    )(info, bucket_step, q, head, relc, w_mine, w_other, own, b1, b2, b3, lhs_rows, rel_ids)
    got23 = lax.ppermute(s23, "z", [(i, (i - 2) % 8) for i in range(8)])
    gr = exchange(gr, "x")
    pieces = call(place_kernel, "place", (8, 2 * W, 128), [SM, VM])(info, gr)
    pieces, got23 = lax.optimization_barrier((pieces, got23))
    carry = call(carry_kernel, "carry", (4 * W, ROWS), [SM] + [VM] * 2)(info, s1, got23)
    got1 = lax.ppermute(carry, "z", [(i, (i - 1) % 8) for i in range(8)])
    half = call(fold_kernel, "fold", (2 * W, 128), [VM])(exchange(pieces, "z"))
    twin, got1 = lax.optimization_barrier((lax.ppermute(half, "yh", SWAP), got1))
    rel, ring, wrap = call(both_kernel, "both", [(8, 2 * W, 128), block, block], [SM] + [VM] * 5)(info, half, twin, s0, got1, got23)
    wrap = lax.ppermute(wrap, DOM, [(i, (i - 8) % 64) for i in range(64) if i % 8 >= 5])
    rel, wrap = lax.optimization_barrier((exchange(rel, "z"), wrap))
    rel = exchange(call(copies_kernel, "copies", (4, 16 * W, 128), [VM])(rel), "x")
    ent, sq = call(square_kernel, "square", [block, (8, 1, ROWS + REL)], [VM] * 3)(rel, ring, wrap)
    sq = exchange(sq, DIM)
    new_re, new_im, new_acc, new_rel_re, new_rel_im, new_rel_acc = call(
        update_kernel, "update", [(W, ROWS), (W, ROWS), (1, ROWS), (W, REL), (W, REL), (1, REL)], [VM] * 9
    )(sq, rel, ent, ent_re, ent_im, ent_acc.reshape(1, ROWS), rel_re, rel_im, rel_acc.reshape(1, REL))
    return new_re, new_im, new_acc.reshape(ROWS), new_rel_re, new_rel_im, new_rel_acc.reshape(REL)


def solution(mesh):
    fine = Mesh(mesh.devices.reshape(2, 4, 8, 4, 2), DOM + DIM)
    return jax.shard_map(
        per_device,
        mesh=fine,
        in_specs=(
            P(DIM, DOM), P(DIM, DOM), P(DOM), P(DIM, None), P(DIM, None), P(),
            P(DOM, None), P(DOM, None), P(DOM, None), P(DOM, None), P(DOM),
        ),
        out_specs=(P(DIM, DOM), P(DIM, DOM), P(DOM), P(DIM, None), P(DIM, None), P()),
        check_vma=False,
    )
```

```python
import jax
import jax.numpy as jnp
from jax import lax
from jax.experimental import pallas as pl
from jax.experimental.pallas import tpu as pltpu
from jax.sharding import Mesh, PartitionSpec as P

D = 400
STEPS = 4
LEARN_RATE = 0.1
W = 25
ROWS = 512
CH = 128
REL = 4096
DOM = ("yh", "x", "z")
DIM = ("yl", "core")
NEAR = {True}
FAR = {False}
SWAP = [(0, 1), (1, 0)]
F32 = jnp.float32
BF16 = jnp.bfloat16
I32 = jnp.int32
HIGHEST = lax.Precision.HIGHEST
VM = pl.BlockSpec(memory_space=pltpu.VMEM)
SM = pl.BlockSpec(memory_space=pltpu.SMEM)


def call(kernel, name, outs, specs):
    single = isinstance(outs, tuple)
    shapes = [jax.ShapeDtypeStruct(s, F32) for s in ([outs] if single else outs)]
    return pl.pallas_call(
        kernel,
        out_shape=shapes[0] if single else shapes,
        in_specs=specs,
        out_specs=VM if single else [VM] * len(shapes),
        compiler_params=pltpu.CompilerParams(vmem_limit_bytes=32 * 1024 * 1024),
        name=name,
    )


def iota(shape, axis):
    return lax.broadcasted_iota(I32, shape, axis)


def split3(x):
    hi = x.astype(BF16)
    rest = x - hi.astype(F32)
    mid = rest.astype(BF16)
    lo = (rest - mid.astype(F32)).astype(BF16)
    return jnp.concatenate([hi, mid, lo], 0)


def join3(y):
    r = y.shape[0] // 3
    return y[:r] + (y[r : 2 * r] + y[2 * r :])


def nn(a, b):
    return lax.dot_general(a, b, (((1,), (0,)), ((), ())), preferred_element_type=F32)


def nt(a, b):
    return lax.dot_general(a, b, (((1,), (1,)), ((), ())), preferred_element_type=F32)


def onehot_rows(ids, count):
    return jnp.where(iota((count, ids.shape[1]), 0) == ids, 1.0, 0.0).astype(BF16)


def pad32(x):
    return jnp.concatenate([x, jnp.zeros((32 - W, x.shape[1]), F32)], 0)


def pack(block):
    return jnp.concatenate([pad32(block[:W]), pad32(block[W:])], 0)


def edge_ids(ref):
    return jnp.concatenate([ref[0:1, :], ref[1:2, :]], 1)


def query_kernel(info, ent_re, ent_im, rel_re, rel_im, lhs, rhs, rel_ids, neg, eacc, head_o, relc_o, q_o, m_o, hit_o, eacc_o):
    eacc_o[...] = eacc[...]
    own = jnp.concatenate([pad32(ent_re[...]), pad32(ent_im[...])], 0)
    head = join3(nn(split3(own), onehot_rows(edge_ids(lhs), ROWS)))
    ids = edge_ids(rel_ids)
    step = 1024
    acc = jnp.zeros((192, 2 * CH), F32)
    for k in range(0, REL, step):
        part = jnp.concatenate([pad32(rel_re[:, k : k + step]), pad32(rel_im[:, k : k + step])], 0)
        acc = acc + nn(split3(part), onehot_rows(ids - k, step))
    relc = join3(acc)
    head_o[...] = head
    relc_o[...] = relc
    h_re, h_im = head[:32], head[32:]
    r_re, r_im = relc[:32], relc[32:]
    q_o[...] = jnp.concatenate([h_re * r_re - h_im * r_im, h_re * r_im + h_im * r_re], 0)
    first = info[0] == 0
    ones = jnp.ones((16, neg.shape[1]), BF16)
    m_o[...] = nt(ones, onehot_rows(jnp.where(first, neg[0:1, :], neg[1:2, :]), ROWS))[:8]
    ids = jnp.where(first, rhs[0:1, :], rhs[1:2, :])
    hit_o[...] = jnp.transpose(jnp.where(iota((ROWS, CH), 0) == ids, 1.0, 0.0))


def choose(step, blocks):
    b = blocks[STEPS - 1]
    for s in range(STEPS - 1):
        b = jnp.where(step == s, blocks[s], b)
    return b


def score_kernel(info, bucket, q_r, b0, near1, near2, b3, far2, far1, keep_o, send_o, b1_o, b2_o):
    core = info[0]
    b1_o[...] = jnp.where(info[4] < 1, far1[...], near1[...])
    b2_o[...] = jnp.where(info[4] < 2, far2[...], near2[...])
    blocks = [pack(b[...]) for b in (b0, b1_o, b2_o, b3)]
    q = [q_r[:, 0:CH], q_r[:, CH : 2 * CH]]
    for first, out in ((1, send_o), (0, keep_o)):
        c = core ^ first
        s = lax.dot_general(
            jnp.where(c == 0, q[0], q[1]), choose(bucket[c], blocks),
            (((0,), (0,)), ((), ())), precision=HIGHEST, preferred_element_type=F32)
        for yl in range(4):
            out[yl] = s[32 * yl : 32 * yl + 32]


def add_kernel(a, b, o):
    o[...] = a[...] + b[...]


def weight_kernel(info, bucket, parts, m_r, hit_r, w_o):
    s = parts[0]
    for i in range(1, 4):
        s = s + parts[i]
    m = m_r[0:1, :]
    live = jnp.where(jnp.where(info[0] == 0, bucket[0], bucket[1]) < STEPS, 1.0, 0.0)
    hit = hit_r[pl.ds(pl.multiple_of(info[2] * 32, 32), 32), :] > 0.5
    pos = jnp.sum(jnp.where(hit, s, 0.0), 1, keepdims=True)
    masked = jnp.where(m > 0.0, s, -1e30)
    top = jnp.maximum(jnp.max(masked, 1, keepdims=True), pos)
    e_pos = jnp.exp(pos - top)
    e_neg = m * jnp.exp(masked - top)
    denom = e_pos + jnp.sum(e_neg, 1, keepdims=True)
    w_pos = (e_pos / denom - 1.0) * live
    w = e_neg * (live / denom) + jnp.where(hit, w_pos, 0.0)
    for i in range(4):
        w_o[i] = w


def grad_kernel(info, bucket, q_r, head_r, relc_r, w_mine, w_other, b0, b1, b2, b3, lhs, rel_ids, s0_o, s1_o, s2_o, s3_o, gr_o):
    core = info[0]
    mine = w_mine[...].reshape(CH, ROWS)
    other = w_other[...].reshape(CH, ROWS)
    blocks = [pack(b[...]) for b in (b0, b1, b2, b3)]
    gq = []
    slots = [jnp.zeros((64, ROWS), F32) for _ in range(STEPS)]
    for c in range(2):
        w = jnp.where(core == c, mine, other)
        step = jnp.minimum(bucket[c], STEPS - 1)
        block = choose(step, blocks)
        gq.append(lax.dot_general(block, w, (((1,), (1,)), ((), ())), precision=HIGHEST, preferred_element_type=F32))
        g = lax.dot_general(q_r[:, c * CH : (c + 1) * CH], w, (((1,), (0,)), ((), ())), precision=HIGHEST, preferred_element_type=F32)
        for s in range(STEPS):
            slots[s] = slots[s] + jnp.where(step == s, g, 0.0)
    gq = jnp.concatenate(gq, 1)
    g_re, g_im = gq[:32], gq[32:]
    h_re, h_im = head_r[:32, :], head_r[32:, :]
    r_re, r_im = relc_r[:32, :], relc_r[32:, :]
    gh = jnp.concatenate([g_re * r_re + g_im * r_im, g_im * r_re - g_re * r_im], 0)
    slots[0] = slots[0] + join3(nt(split3(gh), onehot_rows(edge_ids(lhs), ROWS)))
    gr_re = (g_re * h_re + g_im * h_im)[:W]
    gr_im = (g_im * h_re - g_re * h_im)[:W]
    ids = edge_ids(rel_ids).astype(F32)
    for i in range(4):
        gr_o[i, 0:W, :] = gr_re
        gr_o[i, W : 2 * W, :] = gr_im
        gr_o[i, 2 * W : 2 * W + 1, :] = ids
    for ref, slot in zip((s0_o, s1_o, s2_o, s3_o), slots):
        ref[0:W, :] = slot[:W]
        ref[W : 2 * W, :] = slot[32 : 32 + W]


def place_kernel(info, gr, out):
    x = info[1]
    vals = []
    cols = []
    for i in range(4):
        vals.append(split3(pack(gr[i, 0 : 2 * W, :])))
        ids = gr[i, 2 * W : 2 * W + 1, :].astype(I32)
        cols.append(jnp.where(jnp.right_shift(ids, 10) == x, jnp.bitwise_and(ids, 1023), -1))
    total = join3(nt(jnp.concatenate(vals, 1), onehot_rows(jnp.concatenate(cols, 1), 1024)))
    for z in range(8):
        out[z, 0:W, :] = total[:W, 128 * z : 128 * z + 128]
        out[z, W : 2 * W, :] = total[32 : 32 + W, 128 * z : 128 * z + 128]


def fold_kernel(parts, out):
    tot = parts[0]
    for i in range(1, 8):
        tot = tot + parts[i]
    out[...] = tot


def both_kernel(a, b, out):
    tot = a[...] + b[...]
    for i in range(8):
        out[i] = tot


def ring_kernel(info, s0, got1, got2, got3, ring_o, wrap_o):
    z = info[3]
    ring = s0[...]
    wrap = jnp.zeros_like(ring)
    for d, got in ((1, got1), (2, got2), (3, got3)):
        ring = ring + jnp.where(z + d < 8, got[...], 0.0)
        wrap = wrap + jnp.where(z + d < 8, 0.0, got[...])
    ring_o[...] = ring
    wrap_o[...] = wrap


def copies_kernel(a, out):
    for x in range(4):
        for z in range(8):
            out[x, 2 * W * z : 2 * W * z + 2 * W, :] = a[z]


def square_kernel(rel, ring, wrap, ent_o, sq_o):
    ent = ring[...] + wrap[...]
    ent_o[...] = ent
    es = jnp.sum(ent * ent, 0, keepdims=True)
    for i in range(8):
        sq_o[i, :, 0:ROWS] = es
    for t in range(32):
        tot = rel[t // 8, 2 * W * (t % 8) : 2 * W * (t % 8) + 2 * W, :]
        rs = jnp.sum(tot * tot, 0, keepdims=True)
        for i in range(8):
            sq_o[i, :, ROWS + 128 * t : ROWS + 128 * t + 128] = rs


def update_kernel(sq, rel, ent, ent_re, ent_im, eacc, rel_re, rel_im, racc, re_o, im_o, acc_o, rre_o, rim_o, racc_o):
    s = sq[0]
    for i in range(1, 8):
        s = s + sq[i]
    acc = eacc[...] + s[:, :ROWS] / D
    acc_o[...] = acc
    scale = LEARN_RATE / jnp.sqrt(acc)
    re_o[...] = ent_re[...] - scale * ent[0:W, :]
    im_o[...] = ent_im[...] - scale * ent[W : 2 * W, :]
    acc = racc[...] + s[:, ROWS:] / D
    racc_o[...] = acc
    scale = LEARN_RATE / jnp.sqrt(acc)
    for t in range(32):
        at = slice(128 * t, 128 * t + 128)
        tot = rel[t // 8, 2 * W * (t % 8) : 2 * W * (t % 8) + 2 * W, :]
        rre_o[:, at] = rel_re[:, at] - scale[:, at] * tot[:W]
        rim_o[:, at] = rel_im[:, at] - scale[:, at] * tot[W:]


def shift(block, distance, kinds):
    ends = [(i, (i + distance) % 64) for i in range(64)]
    return lax.ppermute(block, DOM, [(i, j) for i, j in ends if (i // 32 == j // 32) in kinds])


def exchange(pieces, axes):
    return lax.all_to_all(pieces, axes, 0, 0)


def per_device(ent_re, ent_im, ent_acc, rel_re, rel_im, rel_acc, lhs_rows, rhs_rows, rel_ids, neg_rows, bucket_step):
    info = jnp.stack([lax.axis_index("core"), lax.axis_index("x"), lax.axis_index("yl"), lax.axis_index("z"), lax.axis_index(("x", "z"))]).astype(I32)
    own = jnp.concatenate([ent_re, ent_im], 0)
    near1, near2, all3 = shift(own, 1, NEAR), shift(own, 2, NEAR), shift(own, 3, NEAR | FAR)
    far2, far1 = shift(own, 2, FAR), shift(own, 1, FAR)
    neg = jnp.pad(neg_rows, ((0, 0), (0, 24)), constant_values=-1)
    head, relc, q, m, hit, eacc = call(
        query_kernel, "query", [(64, 256), (64, 256), (64, 256), (8, ROWS), (CH, ROWS), (1, ROWS)], [SM] + [VM] * 9,
    )(info, ent_re, ent_im, rel_re, rel_im, lhs_rows, rhs_rows, rel_ids, neg, ent_acc.reshape(1, ROWS))
    quarter = (4, 32, ROWS)
    block = (2 * W, ROWS)
    keep, send, b1, b2 = call(
        score_kernel, "score", [quarter, quarter, block, block], [SM, SM] + [VM] * 7
    )(info, bucket_step, q, own, near1, near2, all3, far2, far1)
    s = call(add_kernel, "add", quarter, [VM] * 2)(keep, lax.ppermute(send, "core", SWAP))
    s = exchange(s, "yl")
    w = call(weight_kernel, "weight", quarter, [SM, SM] + [VM] * 3)(info, bucket_step, s, m, hit)
    w_mine = exchange(w, "yl")
    w_other = lax.ppermute(w_mine, "core", SWAP)
    s0, s1, s2, s3, gr = call(
        grad_kernel, "grad", [block, block, block, block, (4, 2 * W + 1, 256)], [SM, SM] + [VM] * 11,
    )(info, bucket_step, q, head, relc, w_mine, w_other, own, b1, b2, all3, lhs_rows, rel_ids)
    got1, got2, got3 = [lax.ppermute(v, "z", [(i, (i - d) % 8) for i in range(8)]) for d, v in ((1, s1), (2, s2), (3, s3))]
    gr = exchange(gr, "x")
    pieces = call(place_kernel, "place", (8, 2 * W, 128), [SM, VM])(info, gr)
    pieces, got1 = lax.optimization_barrier((pieces, got1))
    half = call(fold_kernel, "fold", (2 * W, 128), [VM])(exchange(pieces, "z"))
    ring, wrap = call(ring_kernel, "ring", [block, block], [SM] + [VM] * 4)(info, s0, got1, got2, got3)
    twin, wrap = lax.optimization_barrier((lax.ppermute(half, "yh", SWAP), wrap))
    rel = call(both_kernel, "both", (8, 2 * W, 128), [VM] * 2)(half, twin)
    wrap = lax.ppermute(wrap, DOM, [(i, (i - 8) % 64) for i in range(64) if i % 8 >= 5])
    rel = call(copies_kernel, "copies", (4, 16 * W, 128), [VM])(exchange(rel, "z"))
    rel, wrap = lax.optimization_barrier((rel, wrap))
    rel = exchange(rel, "x")
    ent, sq = call(square_kernel, "square", [block, (8, 1, ROWS + REL)], [VM] * 3)(rel, ring, wrap)
    sq = exchange(sq, DIM)
    new_re, new_im, new_acc, new_rel_re, new_rel_im, new_rel_acc = call(
        update_kernel, "update", [(W, ROWS), (W, ROWS), (1, ROWS), (W, REL), (W, REL), (1, REL)], [VM] * 9
    )(sq, rel, ent, ent_re, ent_im, eacc, rel_re, rel_im, rel_acc.reshape(1, REL))
    return new_re, new_im, new_acc.reshape(ROWS), new_rel_re, new_rel_im, new_rel_acc.reshape(REL)


def solution(mesh):
    fine = Mesh(mesh.devices.reshape(2, 4, 8, 4, 2), DOM + DIM)
    return jax.shard_map(
        per_device,
        mesh=fine,
        in_specs=(
            P(DIM, DOM), P(DIM, DOM), P(DOM), P(DIM, None), P(DIM, None), P(),
            P(DOM, None), P(DOM, None), P(DOM, None), P(DOM, None), P(DOM),
        ),
        out_specs=(P(DIM, DOM), P(DIM, DOM), P(DOM), P(DIM, None), P(DIM, None), P()),
        check_vma=False,
    )
```

```python
import jax
import jax.numpy as jnp
from jax import lax
from jax.experimental import pallas as pl
from jax.experimental.pallas import tpu as pltpu
from jax.sharding import Mesh, PartitionSpec as P

D = 400
STEPS = 4
LEARN_RATE = 0.1
W = 25
ROWS = 512
CH = 128
REL = 4096
DOM = ("yh", "x", "z")
DIM = ("yl", "core")
NEAR = {True}
FAR = {False}
SWAP = [(0, 1), (1, 0)]
F32 = jnp.float32
BF16 = jnp.bfloat16
I32 = jnp.int32
HIGHEST = lax.Precision.HIGHEST
VM = pl.BlockSpec(memory_space=pltpu.VMEM)
SM = pl.BlockSpec(memory_space=pltpu.SMEM)


def call(kernel, name, outs, specs):
    single = isinstance(outs, tuple)
    shapes = [jax.ShapeDtypeStruct(s, F32) for s in ([outs] if single else outs)]
    return pl.pallas_call(
        kernel,
        out_shape=shapes[0] if single else shapes,
        in_specs=specs,
        out_specs=VM if single else [VM] * len(shapes),
        compiler_params=pltpu.CompilerParams(vmem_limit_bytes=32 * 1024 * 1024),
        name=name,
    )


def iota(shape, axis):
    return lax.broadcasted_iota(I32, shape, axis)


def split3(x):
    hi = x.astype(BF16)
    rest = x - hi.astype(F32)
    mid = rest.astype(BF16)
    lo = (rest - mid.astype(F32)).astype(BF16)
    return jnp.concatenate([hi, mid, lo], 0)


def join3(y):
    r = y.shape[0] // 3
    return y[:r] + (y[r : 2 * r] + y[2 * r :])


def nn(a, b):
    return lax.dot_general(a, b, (((1,), (0,)), ((), ())), preferred_element_type=F32)


def nt(a, b):
    return lax.dot_general(a, b, (((1,), (1,)), ((), ())), preferred_element_type=F32)


def onehot_rows(ids, count):
    return jnp.where(iota((count, ids.shape[1]), 0) == ids, 1.0, 0.0).astype(BF16)


def pad32(x):
    return jnp.concatenate([x, jnp.zeros((32 - W, x.shape[1]), F32)], 0)


def pack(block):
    return jnp.concatenate([pad32(block[:W]), pad32(block[W:])], 0)


def edge_ids(ref):
    return jnp.concatenate([ref[0:1, :], ref[1:2, :]], 1)


def query_kernel(info, ent_re, ent_im, rel_re, rel_im, lhs, rhs, rel_ids, neg, eacc, head_o, relc_o, q_o, m_o, hit_o, eacc_o):
    eacc_o[...] = eacc[...]
    own = jnp.concatenate([pad32(ent_re[...]), pad32(ent_im[...])], 0)
    head = join3(nn(split3(own), onehot_rows(edge_ids(lhs), ROWS)))
    ids = edge_ids(rel_ids)
    step = 1024
    acc = jnp.zeros((192, 2 * CH), F32)
    for k in range(0, REL, step):
        part = jnp.concatenate([pad32(rel_re[:, k : k + step]), pad32(rel_im[:, k : k + step])], 0)
        acc = acc + nn(split3(part), onehot_rows(ids - k, step))
    relc = join3(acc)
    head_o[...] = head
    relc_o[...] = relc
    h_re, h_im = head[:32], head[32:]
    r_re, r_im = relc[:32], relc[32:]
    q_o[...] = jnp.concatenate([h_re * r_re - h_im * r_im, h_re * r_im + h_im * r_re], 0)
    first = info[0] == 0
    ones = jnp.ones((16, neg.shape[1]), BF16)
    m_o[...] = nt(ones, onehot_rows(jnp.where(first, neg[0:1, :], neg[1:2, :]), ROWS))[:8]
    ids = jnp.where(first, rhs[0:1, :], rhs[1:2, :])
    hit_o[...] = jnp.transpose(jnp.where(iota((ROWS, CH), 0) == ids, 1.0, 0.0))


def choose(step, blocks):
    b = blocks[STEPS - 1]
    for s in range(STEPS - 1):
        b = jnp.where(step == s, blocks[s], b)
    return b


def score_kernel(info, bucket, q_r, b0, near1, near2, b3, far2, far1, keep_o, send_o, b1_o, b2_o):
    core = info[0]
    b1_o[...] = jnp.where(info[4] < 1, far1[...], near1[...])
    b2_o[...] = jnp.where(info[4] < 2, far2[...], near2[...])
    blocks = [pack(b[...]) for b in (b0, b1_o, b2_o, b3)]
    q = [q_r[:, 0:CH], q_r[:, CH : 2 * CH]]
    for first, out in ((1, send_o), (0, keep_o)):
        c = core ^ first
        s = lax.dot_general(
            jnp.where(c == 0, q[0], q[1]), choose(bucket[c], blocks),
            (((0,), (0,)), ((), ())), precision=HIGHEST, preferred_element_type=F32)
        for yl in range(4):
            out[yl] = s[32 * yl : 32 * yl + 32]


def add_kernel(a, b, o):
    o[...] = a[...] + b[...]


def weight_kernel(info, bucket, parts, m_r, hit_r, w_o):
    s = parts[0]
    for i in range(1, 4):
        s = s + parts[i]
    m = m_r[0:1, :]
    live = jnp.where(jnp.where(info[0] == 0, bucket[0], bucket[1]) < STEPS, 1.0, 0.0)
    hit = hit_r[pl.ds(pl.multiple_of(info[2] * 32, 32), 32), :] > 0.5
    pos = jnp.sum(jnp.where(hit, s, 0.0), 1, keepdims=True)
    masked = jnp.where(m > 0.0, s, -1e30)
    top = jnp.maximum(jnp.max(masked, 1, keepdims=True), pos)
    e_pos = jnp.exp(pos - top)
    e_neg = m * jnp.exp(masked - top)
    denom = e_pos + jnp.sum(e_neg, 1, keepdims=True)
    w_pos = (e_pos / denom - 1.0) * live
    w = e_neg * (live / denom) + jnp.where(hit, w_pos, 0.0)
    for i in range(4):
        w_o[i] = w


def group_grads(c, bucket, q_r, w, b0, b1, b2, b3):
    step = jnp.minimum(jnp.where(c == 0, bucket[0], bucket[1]), STEPS - 1)
    block = choose(step, [pack(b[...]) for b in (b0, b1, b2, b3)])
    query = jnp.where(c == 0, q_r[:, 0:CH], q_r[:, CH : 2 * CH])
    gq = lax.dot_general(block, w, (((1,), (1,)), ((), ())), precision=HIGHEST, preferred_element_type=F32)
    return step, gq, lax.dot_general(query, w, (((1,), (0,)), ((), ())), precision=HIGHEST, preferred_element_type=F32)


def mine_kernel(info, bucket, q_r, w_mine, b0, b1, b2, b3, gq_o, g_o):
    _, gq_o[...], g_o[...] = group_grads(info[0], bucket, q_r, w_mine[...].reshape(CH, ROWS), b0, b1, b2, b3)


def grad_kernel(info, bucket, q_r, head_r, relc_r, gq_mine, g_mine, w_other, b0, b1, b2, b3, lhs, rel_ids, s0_o, s1_o, s2_o, s3_o, gr_o):
    core = info[0]
    step, gq, g = group_grads(1 - core, bucket, q_r, w_other[...].reshape(CH, ROWS), b0, b1, b2, b3)
    own_step = jnp.minimum(jnp.where(core == 0, bucket[0], bucket[1]), STEPS - 1)
    slots = [jnp.where(own_step == s, g_mine[...], 0.0) + jnp.where(step == s, g, 0.0) for s in range(STEPS)]
    mine = gq_mine[...]
    gq = jnp.concatenate([jnp.where(core == 0, mine, gq), jnp.where(core == 0, gq, mine)], 1)
    g_re, g_im = gq[:32], gq[32:]
    h_re, h_im = head_r[:32, :], head_r[32:, :]
    r_re, r_im = relc_r[:32, :], relc_r[32:, :]
    gh = jnp.concatenate([g_re * r_re + g_im * r_im, g_im * r_re - g_re * r_im], 0)
    slots[0] = slots[0] + join3(nt(split3(gh), onehot_rows(edge_ids(lhs), ROWS)))
    gr_re = (g_re * h_re + g_im * h_im)[:W]
    gr_im = (g_im * h_re - g_re * h_im)[:W]
    ids = edge_ids(rel_ids).astype(F32)
    for i in range(4):
        gr_o[i, 0:W, :] = gr_re
        gr_o[i, W : 2 * W, :] = gr_im
        gr_o[i, 2 * W : 2 * W + 1, :] = ids
    for ref, slot in zip((s0_o, s1_o, s2_o, s3_o), slots):
        ref[0:W, :] = slot[:W]
        ref[W : 2 * W, :] = slot[32 : 32 + W]


def place_kernel(info, gr, out):
    x = info[1]
    vals = []
    cols = []
    for i in range(4):
        vals.append(split3(pack(gr[i, 0 : 2 * W, :])))
        ids = gr[i, 2 * W : 2 * W + 1, :].astype(I32)
        cols.append(jnp.where(jnp.right_shift(ids, 10) == x, jnp.bitwise_and(ids, 1023), -1))
    total = join3(nt(jnp.concatenate(vals, 1), onehot_rows(jnp.concatenate(cols, 1), 1024)))
    for z in range(8):
        out[z, 0:W, :] = total[:W, 128 * z : 128 * z + 128]
        out[z, W : 2 * W, :] = total[32 : 32 + W, 128 * z : 128 * z + 128]


def fold_kernel(parts, out):
    tot = parts[0]
    for i in range(1, 8):
        tot = tot + parts[i]
    out[...] = tot


def both_kernel(a, b, out):
    tot = a[...] + b[...]
    for i in range(8):
        out[i] = tot


def ring_kernel(info, s0, got1, got2, got3, ring_o, wrap_o):
    z = info[3]
    ring = s0[...]
    wrap = jnp.zeros_like(ring)
    for d, got in ((1, got1), (2, got2), (3, got3)):
        ring = ring + jnp.where(z + d < 8, got[...], 0.0)
        wrap = wrap + jnp.where(z + d < 8, 0.0, got[...])
    ring_o[...] = ring
    wrap_o[...] = wrap


def copies_kernel(a, out):
    for x in range(4):
        for z in range(8):
            out[x, 2 * W * z : 2 * W * z + 2 * W, :] = a[z]


def square_kernel(rel, ring, wrap, ent_o, sq_o):
    ent = ring[...] + wrap[...]
    ent_o[...] = ent
    es = jnp.sum(ent * ent, 0, keepdims=True)
    for i in range(8):
        sq_o[i, :, 0:ROWS] = es
    for t in range(32):
        tot = rel[t // 8, 2 * W * (t % 8) : 2 * W * (t % 8) + 2 * W, :]
        rs = jnp.sum(tot * tot, 0, keepdims=True)
        for i in range(8):
            sq_o[i, :, ROWS + 128 * t : ROWS + 128 * t + 128] = rs


def update_kernel(sq, rel, ent, ent_re, ent_im, eacc, rel_re, rel_im, racc, re_o, im_o, acc_o, rre_o, rim_o, racc_o):
    s = sq[0]
    for i in range(1, 8):
        s = s + sq[i]
    acc = eacc[...] + s[:, :ROWS] / D
    acc_o[...] = acc
    scale = LEARN_RATE / jnp.sqrt(acc)
    re_o[...] = ent_re[...] - scale * ent[0:W, :]
    im_o[...] = ent_im[...] - scale * ent[W : 2 * W, :]
    acc = racc[...] + s[:, ROWS:] / D
    racc_o[...] = acc
    scale = LEARN_RATE / jnp.sqrt(acc)
    for t in range(32):
        at = slice(128 * t, 128 * t + 128)
        tot = rel[t // 8, 2 * W * (t % 8) : 2 * W * (t % 8) + 2 * W, :]
        rre_o[:, at] = rel_re[:, at] - scale[:, at] * tot[:W]
        rim_o[:, at] = rel_im[:, at] - scale[:, at] * tot[W:]


def shift(block, distance, kinds):
    ends = [(i, (i + distance) % 64) for i in range(64)]
    return lax.ppermute(block, DOM, [(i, j) for i, j in ends if (i // 32 == j // 32) in kinds])


def exchange(pieces, axes):
    return lax.all_to_all(pieces, axes, 0, 0)


def per_device(ent_re, ent_im, ent_acc, rel_re, rel_im, rel_acc, lhs_rows, rhs_rows, rel_ids, neg_rows, bucket_step):
    info = jnp.stack([lax.axis_index("core"), lax.axis_index("x"), lax.axis_index("yl"), lax.axis_index("z"), lax.axis_index(("x", "z"))]).astype(I32)
    own = jnp.concatenate([ent_re, ent_im], 0)
    near1, near2, all3 = shift(own, 1, NEAR), shift(own, 2, NEAR), shift(own, 3, NEAR | FAR)
    far2, far1 = shift(own, 2, FAR), shift(own, 1, FAR)
    neg = jnp.pad(neg_rows, ((0, 0), (0, 24)), constant_values=-1)
    head, relc, q, m, hit, eacc = call(
        query_kernel, "query", [(64, 256), (64, 256), (64, 256), (8, ROWS), (CH, ROWS), (1, ROWS)], [SM] + [VM] * 9,
    )(info, ent_re, ent_im, rel_re, rel_im, lhs_rows, rhs_rows, rel_ids, neg, ent_acc.reshape(1, ROWS))
    quarter = (4, 32, ROWS)
    block = (2 * W, ROWS)
    keep, send, b1, b2 = call(
        score_kernel, "score", [quarter, quarter, block, block], [SM, SM] + [VM] * 7
    )(info, bucket_step, q, own, near1, near2, all3, far2, far1)
    s = call(add_kernel, "add", quarter, [VM] * 2)(keep, lax.ppermute(send, "core", SWAP))
    s = exchange(s, "yl")
    w = call(weight_kernel, "weight", quarter, [SM, SM] + [VM] * 3)(info, bucket_step, s, m, hit)
    w_mine = exchange(w, "yl")
    w_other = lax.ppermute(w_mine, "core", SWAP)
    gq, g = call(mine_kernel, "mine", [(64, CH), (64, ROWS)], [SM, SM] + [VM] * 6)(info, bucket_step, q, w_mine, own, b1, b2, all3)
    s0, s1, s2, s3, gr = call(
        grad_kernel, "grad", [block, block, block, block, (4, 2 * W + 1, 256)], [SM, SM] + [VM] * 12,
    )(info, bucket_step, q, head, relc, gq, g, w_other, own, b1, b2, all3, lhs_rows, rel_ids)
    got1, got2, got3 = [lax.ppermute(v, "z", [(i, (i - d) % 8) for i in range(8)]) for d, v in ((1, s1), (2, s2), (3, s3))]
    gr = exchange(gr, "x")
    pieces = call(place_kernel, "place", (8, 2 * W, 128), [SM, VM])(info, gr)
    pieces, got1 = lax.optimization_barrier((pieces, got1))
    half = call(fold_kernel, "fold", (2 * W, 128), [VM])(exchange(pieces, "z"))
    ring, wrap = call(ring_kernel, "ring", [block, block], [SM] + [VM] * 4)(info, s0, got1, got2, got3)
    twin, wrap = lax.optimization_barrier((lax.ppermute(half, "yh", SWAP), wrap))
    rel = call(both_kernel, "both", (8, 2 * W, 128), [VM] * 2)(half, twin)
    wrap = lax.ppermute(wrap, DOM, [(i, (i - 8) % 64) for i in range(64) if i % 8 >= 5])
    rel = call(copies_kernel, "copies", (4, 16 * W, 128), [VM])(exchange(rel, "z"))
    rel, wrap = lax.optimization_barrier((rel, wrap))
    rel = exchange(rel, "x")
    ent, sq = call(square_kernel, "square", [block, (8, 1, ROWS + REL)], [VM] * 3)(rel, ring, wrap)
    sq = exchange(sq, DIM)
    new_re, new_im, new_acc, new_rel_re, new_rel_im, new_rel_acc = call(
        update_kernel, "update", [(W, ROWS), (W, ROWS), (1, ROWS), (W, REL), (W, REL), (1, REL)], [VM] * 9
    )(sq, rel, ent, ent_re, ent_im, eacc, rel_re, rel_im, rel_acc.reshape(1, REL))
    return new_re, new_im, new_acc.reshape(ROWS), new_rel_re, new_rel_im, new_rel_acc.reshape(REL)


def solution(mesh):
    fine = Mesh(mesh.devices.reshape(2, 4, 8, 4, 2), DOM + DIM)
    return jax.shard_map(
        per_device,
        mesh=fine,
        in_specs=(
            P(DIM, DOM), P(DIM, DOM), P(DOM), P(DIM, None), P(DIM, None), P(),
            P(DOM, None), P(DOM, None), P(DOM, None), P(DOM, None), P(DOM),
        ),
        out_specs=(P(DIM, DOM), P(DIM, DOM), P(DOM), P(DIM, None), P(DIM, None), P()),
        check_vma=False,
    )
```

```python
import jax
import jax.numpy as jnp
from jax import lax
from jax.experimental import pallas as pl
from jax.experimental.pallas import tpu as pltpu
from jax.sharding import Mesh, PartitionSpec as P

D = 400
STEPS = 4
LEARN_RATE = 0.1
W = 25
ROWS = 512
CH = 128
REL = 4096
DOM = ("yh", "x", "z")
DIM = ("yl", "core")
NEAR = {True}
FAR = {False}
SWAP = [(0, 1), (1, 0)]
F32 = jnp.float32
BF16 = jnp.bfloat16
I32 = jnp.int32
HIGHEST = lax.Precision.HIGHEST
VM = pl.BlockSpec(memory_space=pltpu.VMEM)
SM = pl.BlockSpec(memory_space=pltpu.SMEM)


def call(kernel, name, outs, specs):
    single = isinstance(outs, tuple)
    shapes = [jax.ShapeDtypeStruct(s, F32) for s in ([outs] if single else outs)]
    return pl.pallas_call(
        kernel,
        out_shape=shapes[0] if single else shapes,
        in_specs=specs,
        out_specs=VM if single else [VM] * len(shapes),
        compiler_params=pltpu.CompilerParams(vmem_limit_bytes=32 * 1024 * 1024),
        name=name,
    )


def iota(shape, axis):
    return lax.broadcasted_iota(I32, shape, axis)


def split3(x):
    hi = x.astype(BF16)
    rest = x - hi.astype(F32)
    mid = rest.astype(BF16)
    lo = (rest - mid.astype(F32)).astype(BF16)
    return jnp.concatenate([hi, mid, lo], 0)


def split2(x):
    hi = x.astype(BF16)
    return jnp.concatenate([hi, (x - hi.astype(F32)).astype(BF16)], 0)


def join2(y):
    r = y.shape[0] // 2
    return y[:r] + y[r:]


def join3(y):
    r = y.shape[0] // 3
    return y[:r] + (y[r : 2 * r] + y[2 * r :])


def nn(a, b):
    return lax.dot_general(a, b, (((1,), (0,)), ((), ())), preferred_element_type=F32)


def nt(a, b):
    return lax.dot_general(a, b, (((1,), (1,)), ((), ())), preferred_element_type=F32)


def onehot_rows(ids, count):
    return jnp.where(iota((count, ids.shape[1]), 0) == ids, 1.0, 0.0).astype(BF16)


def pad32(x):
    return jnp.concatenate([x, jnp.zeros((32 - W, x.shape[1]), F32)], 0)


def pack(block):
    return jnp.concatenate([pad32(block[:W]), pad32(block[W:])], 0)


def edge_ids(ref):
    return jnp.concatenate([ref[0:1, :], ref[1:2, :]], 1)


def query_kernel(info, ent_re, ent_im, rel_re, rel_im, lhs, rhs, rel_ids, neg, eacc, head_o, relc_o, q_o, m_o, hit_o, eacc_o):
    eacc_o[...] = eacc[...]
    own = jnp.concatenate([pad32(ent_re[...]), pad32(ent_im[...])], 0)
    head = join3(nn(split3(own), onehot_rows(edge_ids(lhs), ROWS)))
    ids = edge_ids(rel_ids)
    step = 1024
    acc = jnp.zeros((192, 2 * CH), F32)
    for k in range(0, REL, step):
        part = jnp.concatenate([pad32(rel_re[:, k : k + step]), pad32(rel_im[:, k : k + step])], 0)
        acc = acc + nn(split3(part), onehot_rows(ids - k, step))
    relc = join3(acc)
    head_o[...] = head
    relc_o[...] = relc
    h_re, h_im = head[:32], head[32:]
    r_re, r_im = relc[:32], relc[32:]
    q_o[...] = jnp.concatenate([h_re * r_re - h_im * r_im, h_re * r_im + h_im * r_re], 0)
    first = info[0] == 0
    ones = jnp.ones((16, neg.shape[1]), BF16)
    m_o[...] = nt(ones, onehot_rows(jnp.where(first, neg[0:1, :], neg[1:2, :]), ROWS))[:8]
    ids = jnp.where(first, rhs[0:1, :], rhs[1:2, :])
    hit_o[...] = jnp.transpose(jnp.where(iota((ROWS, CH), 0) == ids, 1.0, 0.0))


def choose(step, blocks):
    b = blocks[STEPS - 1]
    for s in range(STEPS - 1):
        b = jnp.where(step == s, blocks[s], b)
    return b


def score_kernel(info, bucket, q_r, b0, near1, near2, b3, far2, far1, keep_o, send_o, b1_o, b2_o):
    core = info[0]
    b1_o[...] = jnp.where(info[4] < 1, far1[...], near1[...])
    b2_o[...] = jnp.where(info[4] < 2, far2[...], near2[...])
    blocks = [pack(b[...]) for b in (b0, b1_o, b2_o, b3)]
    q = [q_r[:, 0:CH], q_r[:, CH : 2 * CH]]
    for first, out in ((1, send_o), (0, keep_o)):
        c = core ^ first
        s = lax.dot_general(
            jnp.where(c == 0, q[0], q[1]), choose(bucket[c], blocks),
            (((0,), (0,)), ((), ())), precision=HIGHEST, preferred_element_type=F32)
        for yl in range(4):
            out[yl] = s[32 * yl : 32 * yl + 32]


def add_kernel(a, b, o):
    o[...] = a[...] + b[...]


def weight_kernel(info, bucket, parts, m_r, hit_r, w_o):
    s = parts[0]
    for i in range(1, 4):
        s = s + parts[i]
    m = m_r[0:1, :]
    live = jnp.where(jnp.where(info[0] == 0, bucket[0], bucket[1]) < STEPS, 1.0, 0.0)
    hit = hit_r[pl.ds(pl.multiple_of(info[2] * 32, 32), 32), :] > 0.5
    pos = jnp.sum(jnp.where(hit, s, 0.0), 1, keepdims=True)
    masked = jnp.where(m > 0.0, s, -1e30)
    top = jnp.maximum(jnp.max(masked, 1, keepdims=True), pos)
    e_pos = jnp.exp(pos - top)
    e_neg = m * jnp.exp(masked - top)
    denom = e_pos + jnp.sum(e_neg, 1, keepdims=True)
    w_pos = (e_pos / denom - 1.0) * live
    w = e_neg * (live / denom) + jnp.where(hit, w_pos, 0.0)
    for i in range(4):
        w_o[i] = w


def grad_kernel(info, bucket, q_r, head_r, relc_r, w_mine, w_other, b0, b1, b2, b3, lhs, rel_ids, s0_o, s1_o, s2_o, s3_o, gr_o):
    core = info[0]
    mine = w_mine[...].reshape(CH, ROWS)
    other = w_other[...].reshape(CH, ROWS)
    blocks = [pack(b[...]) for b in (b0, b1, b2, b3)]
    gq = []
    slots = [jnp.zeros((64, ROWS), F32) for _ in range(STEPS)]
    for c in range(2):
        w = jnp.where(core == c, mine, other)
        step = jnp.minimum(bucket[c], STEPS - 1)
        block = choose(step, blocks)
        gq.append(lax.dot_general(block, w, (((1,), (1,)), ((), ())), precision=HIGHEST, preferred_element_type=F32))
        g = lax.dot_general(q_r[:, c * CH : (c + 1) * CH], w, (((1,), (0,)), ((), ())), precision=HIGHEST, preferred_element_type=F32)
        for s in range(STEPS):
            slots[s] = slots[s] + jnp.where(step == s, g, 0.0)
    gq = jnp.concatenate(gq, 1)
    g_re, g_im = gq[:32], gq[32:]
    h_re, h_im = head_r[:32, :], head_r[32:, :]
    r_re, r_im = relc_r[:32, :], relc_r[32:, :]
    gh = jnp.concatenate([g_re * r_re + g_im * r_im, g_im * r_re - g_re * r_im], 0)
    slots[0] = slots[0] + join2(nt(split2(gh), onehot_rows(edge_ids(lhs), ROWS)))
    gr_re = (g_re * h_re + g_im * h_im)[:W]
    gr_im = (g_im * h_re - g_re * h_im)[:W]
    ids = edge_ids(rel_ids).astype(F32)
    for i in range(4):
        gr_o[i, 0:W, :] = gr_re
        gr_o[i, W : 2 * W, :] = gr_im
        gr_o[i, 2 * W : 2 * W + 1, :] = ids
    for ref, slot in zip((s0_o, s1_o, s2_o, s3_o), slots):
        ref[0:W, :] = slot[:W]
        ref[W : 2 * W, :] = slot[32 : 32 + W]


def place_kernel(info, gr, out):
    x = info[1]
    vals = []
    cols = []
    for i in range(4):
        vals.append(split2(pack(gr[i, 0 : 2 * W, :])))
        ids = gr[i, 2 * W : 2 * W + 1, :].astype(I32)
        cols.append(jnp.where(jnp.right_shift(ids, 10) == x, jnp.bitwise_and(ids, 1023), -1))
    total = join2(nt(jnp.concatenate(vals, 1), onehot_rows(jnp.concatenate(cols, 1), 1024)))
    for z in range(8):
        out[z, 0:W, :] = total[:W, 128 * z : 128 * z + 128]
        out[z, W : 2 * W, :] = total[32 : 32 + W, 128 * z : 128 * z + 128]


def fold_kernel(parts, out):
    tot = parts[0]
    for i in range(1, 8):
        tot = tot + parts[i]
    out[...] = tot


def both_kernel(a, b, out):
    tot = a[...] + b[...]
    for i in range(8):
        out[i] = tot


def ring_kernel(info, s0, got1, got2, got3, ring_o, wrap_o):
    z = info[3]
    ring = s0[...]
    wrap = jnp.zeros_like(ring)
    for d, got in ((1, got1), (2, got2), (3, got3)):
        ring = ring + jnp.where(z + d < 8, got[...], 0.0)
        wrap = wrap + jnp.where(z + d < 8, 0.0, got[...])
    ring_o[...] = ring
    wrap_o[...] = wrap


def copies_kernel(a, out):
    for x in range(4):
        for z in range(8):
            out[x, 2 * W * z : 2 * W * z + 2 * W, :] = a[z]


def square_kernel(rel, ring, wrap, ent_o, sq_o):
    ent = ring[...] + wrap[...]
    ent_o[...] = ent
    es = jnp.sum(ent * ent, 0, keepdims=True)
    for i in range(8):
        sq_o[i, :, 0:ROWS] = es
    for t in range(32):
        tot = rel[t // 8, 2 * W * (t % 8) : 2 * W * (t % 8) + 2 * W, :]
        rs = jnp.sum(tot * tot, 0, keepdims=True)
        for i in range(8):
            sq_o[i, :, ROWS + 128 * t : ROWS + 128 * t + 128] = rs


def update_kernel(sq, rel, ent, ent_re, ent_im, eacc, rel_re, rel_im, racc, re_o, im_o, acc_o, rre_o, rim_o, racc_o):
    s = sq[0]
    for i in range(1, 8):
        s = s + sq[i]
    acc = eacc[...] + s[:, :ROWS] / D
    acc_o[...] = acc
    scale = LEARN_RATE / jnp.sqrt(acc)
    re_o[...] = ent_re[...] - scale * ent[0:W, :]
    im_o[...] = ent_im[...] - scale * ent[W : 2 * W, :]
    acc = racc[...] + s[:, ROWS:] / D
    racc_o[...] = acc
    scale = LEARN_RATE / jnp.sqrt(acc)
    for t in range(32):
        at = slice(128 * t, 128 * t + 128)
        tot = rel[t // 8, 2 * W * (t % 8) : 2 * W * (t % 8) + 2 * W, :]
        rre_o[:, at] = rel_re[:, at] - scale[:, at] * tot[:W]
        rim_o[:, at] = rel_im[:, at] - scale[:, at] * tot[W:]


def shift(block, distance, kinds):
    ends = [(i, (i + distance) % 64) for i in range(64)]
    return lax.ppermute(block, DOM, [(i, j) for i, j in ends if (i // 32 == j // 32) in kinds])


def exchange(pieces, axes):
    return lax.all_to_all(pieces, axes, 0, 0)


def per_device(ent_re, ent_im, ent_acc, rel_re, rel_im, rel_acc, lhs_rows, rhs_rows, rel_ids, neg_rows, bucket_step):
    info = jnp.stack([lax.axis_index("core"), lax.axis_index("x"), lax.axis_index("yl"), lax.axis_index("z"), lax.axis_index(("x", "z"))]).astype(I32)
    own = jnp.concatenate([ent_re, ent_im], 0)
    near1, near2, all3 = shift(own, 1, NEAR), shift(own, 2, NEAR), shift(own, 3, NEAR | FAR)
    far2, far1 = shift(own, 2, FAR), shift(own, 1, FAR)
    neg = jnp.pad(neg_rows, ((0, 0), (0, 24)), constant_values=-1)
    head, relc, q, m, hit, eacc = call(
        query_kernel, "query", [(64, 256), (64, 256), (64, 256), (8, ROWS), (CH, ROWS), (1, ROWS)], [SM] + [VM] * 9,
    )(info, ent_re, ent_im, rel_re, rel_im, lhs_rows, rhs_rows, rel_ids, neg, ent_acc.reshape(1, ROWS))
    quarter = (4, 32, ROWS)
    block = (2 * W, ROWS)
    keep, send, b1, b2 = call(
        score_kernel, "score", [quarter, quarter, block, block], [SM, SM] + [VM] * 7
    )(info, bucket_step, q, own, near1, near2, all3, far2, far1)
    s = call(add_kernel, "add", quarter, [VM] * 2)(keep, lax.ppermute(send, "core", SWAP))
    s = exchange(s, "yl")
    w = call(weight_kernel, "weight", quarter, [SM, SM] + [VM] * 3)(info, bucket_step, s, m, hit)
    w_mine = exchange(w, "yl")
    w_other = lax.ppermute(w_mine, "core", SWAP)
    s0, s1, s2, s3, gr = call(
        grad_kernel, "grad", [block, block, block, block, (4, 2 * W + 1, 256)], [SM, SM] + [VM] * 11,
    )(info, bucket_step, q, head, relc, w_mine, w_other, own, b1, b2, all3, lhs_rows, rel_ids)
    got1, got2, got3 = [lax.ppermute(v, "z", [(i, (i - d) % 8) for i in range(8)]) for d, v in ((1, s1), (2, s2), (3, s3))]
    gr = exchange(gr, "x")
    pieces = call(place_kernel, "place", (8, 2 * W, 128), [SM, VM])(info, gr)
    pieces, got1 = lax.optimization_barrier((pieces, got1))
    half = call(fold_kernel, "fold", (2 * W, 128), [VM])(exchange(pieces, "z"))
    ring, wrap = call(ring_kernel, "ring", [block, block], [SM] + [VM] * 4)(info, s0, got1, got2, got3)
    twin, wrap = lax.optimization_barrier((lax.ppermute(half, "yh", SWAP), wrap))
    rel = call(both_kernel, "both", (8, 2 * W, 128), [VM] * 2)(half, twin)
    wrap = lax.ppermute(wrap, DOM, [(i, (i - 8) % 64) for i in range(64) if i % 8 >= 5])
    rel = call(copies_kernel, "copies", (4, 16 * W, 128), [VM])(exchange(rel, "z"))
    rel, wrap = lax.optimization_barrier((rel, wrap))
    rel = exchange(rel, "x")
    ent, sq = call(square_kernel, "square", [block, (8, 1, ROWS + REL)], [VM] * 3)(rel, ring, wrap)
    sq = exchange(sq, DIM)
    new_re, new_im, new_acc, new_rel_re, new_rel_im, new_rel_acc = call(
        update_kernel, "update", [(W, ROWS), (W, ROWS), (1, ROWS), (W, REL), (W, REL), (1, REL)], [VM] * 9
    )(sq, rel, ent, ent_re, ent_im, eacc, rel_re, rel_im, rel_acc.reshape(1, REL))
    return new_re, new_im, new_acc.reshape(ROWS), new_rel_re, new_rel_im, new_rel_acc.reshape(REL)


def solution(mesh):
    fine = Mesh(mesh.devices.reshape(2, 4, 8, 4, 2), DOM + DIM)
    return jax.shard_map(
        per_device,
        mesh=fine,
        in_specs=(
            P(DIM, DOM), P(DIM, DOM), P(DOM), P(DIM, None), P(DIM, None), P(),
            P(DOM, None), P(DOM, None), P(DOM, None), P(DOM, None), P(DOM),
        ),
        out_specs=(P(DIM, DOM), P(DIM, DOM), P(DOM), P(DIM, None), P(DIM, None), P()),
        check_vma=False,
    )
```
